256 devices in a mesh: ctx: 16 (over x, y_hi, core), tp: 16 (over y_lo, z).
Axes of the slice: x: 4, y: 4 (y_hi: 2, y_lo: 2; y = y_hi * 2 + y_lo), z: 8, core: 2. Of those that a mesh axis runs over, the one named last changes fastest.
Arguments:
- gate_proj: bfloat16 [4096, 4096], P('ctx', 'tp'), may hold values from -6 to 6
- key_proj: bfloat16 [4096, 4096], P('ctx', 'tp'), may hold values from -6 to 6
- value_proj: bfloat16 [4096, 4096], P('ctx', 'tp'), may hold values from -6 to 6
- stream: bfloat16 [4096, 4096], P('ctx', 'tp'), may hold values from -60 to 60
- decay_rate: float32 [16, 4096], P(None, 'tp'), may hold values from 0 to 1
- residue: float32 [16, 4096], P(None, 'tp'), may hold values from -2 to 2
- norm_gain: float32 [4096], P('tp'), may hold values from 0.1 to 1.9
- query_att: bfloat16 [4096, 4096], P('ctx', 'tp'), may hold values from -5 to 5
- key_att: bfloat16 [4096, 4096], P('ctx', 'tp'), may hold values from -5 to 5
- out_grad: bfloat16 [4096, 4096], P('ctx', 'tp'), may hold values from -6 to 6
Outputs:
- attended: bfloat16 [4096, 4096], P('ctx', 'tp')
- gate_grad: bfloat16 [4096, 4096], P('ctx', 'tp')
- keyproj_grad: bfloat16 [4096, 4096], P('ctx', 'tp')
- value_grad: bfloat16 [4096, 4096], P('ctx', 'tp')
- stream_grad: bfloat16 [4096, 4096], P('ctx', 'tp')
- gain_grad: float32 [4096], P('tp')
- query_grad: bfloat16 [4096, 4096], P('ctx', 'tp')
- keyatt_grad: bfloat16 [4096, 4096], P('ctx', 'tp')
The draws below stay inside these ranges and needn't reach their ends.
All inputs are finite; a program needn't handle non-finite values.
Results may differ from the reference program's by a relative error of at most 0.03.
Values may be sent and summed in bfloat16 or wider, within the bound.
A program may use at most 64 MiB of HBM per device.

```python
import jax
import jax.numpy as jnp
from jax import lax

HEADS = 32
HD = 128
MODES = 16
CH = 4096
SEQ = 4096


def shared_rates(key, slow_share):
    pick_key, slow_key, fast_key, mode_key = jax.random.split(key, 4)
    slow = jax.random.uniform(pick_key, (CH,)) < slow_share
    slow_rate = jnp.exp(jax.random.uniform(slow_key, (CH,), minval=jnp.log(0.3 / SEQ), maxval=jnp.log(2.3 / SEQ)))
    fast_rate = jnp.exp(jax.random.uniform(fast_key, (CH,), minval=jnp.log(2.3 / SEQ), maxval=jnp.log(1.0 / 30.0)))
    base_rate = jnp.where(slow, slow_rate, fast_rate)
    spread = jnp.exp(jax.random.uniform(mode_key, (MODES, CH), minval=0.0, maxval=jnp.log(20.0)))
    spread = spread.at[0].set(1.0)
    return base_rate[None, :] * spread


def draw_decay_rate(key, part):
    rates = shared_rates(key, 0.5)
    return rates


def draw_residue(key, part):
    rates = shared_rates(key, 0.5)
    key = jax.random.fold_in(key, 2)
    noise = jnp.clip(jax.random.normal(key, (MODES, CH)), -4.0, 4.0)
    return noise * jnp.sqrt(2.0 * rates / MODES)


def draw_stream(key, part):
    key = jax.random.fold_in(key, 3)
    row_key, jitter_key, base_key = jax.random.split(key, 3)
    row_scale = jnp.exp(jax.random.uniform(row_key, (SEQ, 1), minval=jnp.log(0.3), maxval=jnp.log(3.0)))
    position = jnp.arange(CH, dtype=jnp.float32) / CH
    jitter = 0.3 * jax.random.uniform(jitter_key, (CH,), minval=-1.0, maxval=1.0)
    col_scale = jnp.exp(jnp.log(10.0) * (position - 0.5) + jitter)
    base = jnp.clip(jax.random.normal(base_key, (SEQ, CH)), -4.0, 4.0)
    return (base * row_scale * col_scale[None, :]).astype(jnp.bfloat16)


def draw_query_att(key, part):
    key = jax.random.fold_in(key, 4)
    return jnp.clip(jax.random.normal(key, (SEQ, CH)), -4.0, 4.0).astype(jnp.bfloat16)


def draw_key_att(key, part):
    key = jax.random.fold_in(key, 5)
    return jnp.clip(jax.random.normal(key, (SEQ, CH)), -4.0, 4.0).astype(jnp.bfloat16)


def shard_levels(rng, shape, cuts, smallest, top_value):
    factor_of = 1.0
    for dim, shards_of in cuts:
        draws = jax.random.uniform(jax.random.fold_in(jax.random.fold_in(rng, 6), dim), (shards_of,), jnp.float32, smallest / len(cuts), top_value / len(cuts))
        factor_of = factor_of * jnp.repeat(jnp.exp(draws), shape[dim] // shards_of).reshape((-1,) + (1,) * (len(shape) - 1 - dim))
    return factor_of


def normal_values(own_key, extent, width, limit, shards=(), kind=jnp.bfloat16):
    loudness = shard_levels(own_key, extent, shards, -0.22, 0.18) if shards else 1.0
    values = jax.random.normal(own_key, extent, jnp.float32) * width * loudness
    return jnp.minimum(jnp.maximum(values, -limit), limit).astype(kind)


def setup_inputs(seed: int = 0) -> dict:
    keys = jax.random.split(jax.random.key(seed), 11)
    return {
        "gate_proj": normal_values(keys[0], (SEQ, CH), 1.0, 6.0, ((0, 16), (1, 16))),
        "key_proj": normal_values(keys[1], (SEQ, CH), 1.0, 6.0, ((0, 16), (1, 16))),
        "value_proj": normal_values(keys[2], (SEQ, CH), 1.0, 6.0, ((0, 16), (1, 16))),
        "stream": draw_stream(jax.random.fold_in(keys[10], 71), 0),
        "decay_rate": draw_decay_rate(jax.random.fold_in(keys[10], 71), 0),
        "residue": draw_residue(jax.random.fold_in(keys[10], 71), 0),
        "norm_gain": jnp.clip(1.0 + 0.18 * jax.random.normal(keys[6], (CH,), jnp.float32), 0.1, 1.9),
        "query_att": draw_query_att(jax.random.fold_in(keys[10], 71), 0),
        "key_att": draw_key_att(jax.random.fold_in(keys[10], 71), 0),
        "out_grad": normal_values(keys[9], (SEQ, CH), 1.0, 6.0, ((0, 16), (1, 16))),
    }


NEG_FILL = -1e+30
NORM_EPS = 1e-06

def modal_scan(signal, decay_rate, residue, backward):
    factor = jnp.exp(-decay_rate)

    def advance(running, column):
        running = factor * running + column[None, :]
        return (running, lax.optimization_barrier(jnp.sum(residue * running, axis=0)))
    _, output = lax.scan(advance, jnp.zeros(decay_rate.shape, jnp.float32), signal, reverse=backward)
    return output

def split_heads(array):
    return jnp.transpose(array.reshape(SEQ, HEADS, HD), (1, 0, 2))

def join_heads(array):
    return jnp.transpose(array, (1, 0, 2)).reshape(SEQ, HEADS * HD)

def reference(gate_proj, key_proj, value_proj, stream, decay_rate, residue, norm_gain, query_att, key_att, out_grad):
    mixed = key_proj.astype(jnp.float32) * value_proj.astype(jnp.float32)
    conv = modal_scan(mixed, decay_rate, residue, False)
    gate = gate_proj.astype(jnp.float32)
    summed = stream.astype(jnp.float32) + gate * conv
    inverse = lax.rsqrt(lax.optimization_barrier(jnp.mean(summed * summed, axis=1, keepdims=True)) + NORM_EPS)
    normed = summed * inverse
    values = (normed * norm_gain[None, :]).astype(jnp.bfloat16)
    scale = HD ** (-0.5)
    allowed = jnp.tril(jnp.ones((SEQ, SEQ), dtype=bool))

    def forward_head(operands):
        query_h, key_h, value_h = operands
        scores = jnp.dot(query_h, key_h.T, preferred_element_type=jnp.float32) * scale
        scores = jnp.where(allowed, scores, NEG_FILL)
        top = lax.optimization_barrier(jnp.max(scores, axis=1, keepdims=True))
        exps = jnp.exp(scores - top)
        total = lax.optimization_barrier(jnp.sum(exps, axis=1, keepdims=True))
        output = jnp.dot(exps.astype(jnp.bfloat16), value_h, preferred_element_type=jnp.float32) / total
        return (output.astype(jnp.bfloat16), (top + jnp.log(total))[:, 0])
    query_heads = split_heads(query_att)
    key_heads = split_heads(key_att)
    value_heads = split_heads(values)
    grad_heads = split_heads(out_grad)
    attended_heads, log_total = lax.map(forward_head, (query_heads, key_heads, value_heads))
    attended = join_heads(attended_heads)
    delta = lax.optimization_barrier(jnp.sum(grad_heads.astype(jnp.float32) * attended_heads.astype(jnp.float32), axis=2))

    def backward_head(operands):
        query_h, key_h, value_h, grad_h, total_h, delta_h = operands
        scores = jnp.dot(query_h, key_h.T, preferred_element_type=jnp.float32) * scale
        probs = jnp.where(allowed, jnp.exp(scores - total_h[:, None]), 0.0)
        value_part = jnp.dot(probs.astype(jnp.bfloat16).T, grad_h, preferred_element_type=jnp.float32)
        prob_grad = jnp.dot(grad_h, value_h.T, preferred_element_type=jnp.float32)
        score_grad = (probs * (prob_grad - delta_h[:, None])).astype(jnp.bfloat16)
        query_part = jnp.dot(score_grad, key_h, preferred_element_type=jnp.float32) * scale
        key_part = jnp.dot(score_grad.T, query_h, preferred_element_type=jnp.float32) * scale
        return (query_part, key_part, value_part)
    query_parts, key_parts, value_parts = lax.map(backward_head, (query_heads, key_heads, value_heads, grad_heads, log_total, delta))
    query_grad = join_heads(query_parts).astype(jnp.bfloat16)
    keyatt_grad = join_heads(key_parts).astype(jnp.bfloat16)
    dvalues = join_heads(value_parts)
    gain_grad = lax.optimization_barrier(jnp.sum(dvalues * normed, axis=0))
    dnormed = dvalues * norm_gain[None, :]
    dsummed = inverse * (dnormed - normed * lax.optimization_barrier(jnp.mean(dnormed * normed, axis=1, keepdims=True)))
    stream_grad = dsummed.astype(jnp.bfloat16)
    gate_grad = (dsummed * conv).astype(jnp.bfloat16)
    dmixed = modal_scan(dsummed * gate, decay_rate, residue, True)
    keyproj_grad = (dmixed * value_proj.astype(jnp.float32)).astype(jnp.bfloat16)
    value_grad = (dmixed * key_proj.astype(jnp.float32)).astype(jnp.bfloat16)
    return (attended, gate_grad, keyproj_grad, value_grad, stream_grad, gain_grad, query_grad, keyatt_grad)
```

```python
import jax
import jax.numpy as jnp
from jax import lax
from jax.experimental import pallas as pl
from jax.experimental.pallas import tpu as pltpu
from jax.sharding import PartitionSpec as P

HD = 128
BLK = 256
MODES = 16
CHUNK = 64
NX = 4
FILL = -1e30
EPS = 1e-06
LOG2E = 1.4426950408889634
NT = (((1,), (1,)), ((), ()))
HIGHEST = lax.Precision.HIGHEST
F32 = jnp.float32
BF16 = jnp.bfloat16
Q, DO, K, V = 0, 1, 2, 3
R_DV, R_DK, R_ATT, R_DQ = 0, 1, 2, 3


def remote(src, dst, send, recv, **where):
    return pltpu.make_async_remote_copy(
        src_ref=src,
        dst_ref=dst,
        send_sem=send,
        recv_sem=recv,
        device_id=where,
        device_id_type=pl.DeviceIdType.MESH,
    )


def loop(lo, hi, body):
    def step(i, carry):
        body(i)
        return carry

    lax.fori_loop(lo, hi, step, 0)


def halves(row):
    return jnp.concatenate(
        [jnp.broadcast_to(row[:, :HD], (4, HD)), jnp.broadcast_to(row[:, HD:], (4, HD))], axis=0
    )


def columns(row):
    return jnp.transpose(jnp.broadcast_to(row, (HD, row.shape[1])))


def row_sums(x):
    ones = jnp.ones((8, x.shape[1]), F32)
    return lax.dot_general(ones, x, NT, precision=HIGHEST, preferred_element_type=F32)[0:1]


def dot_nt(a, b):
    return lax.dot_general(a, b, NT, preferred_element_type=F32)


def dot(a, b):
    return jnp.dot(a, b, preferred_element_type=F32)


def kernel(
    n_ctx,
    n_tp,
    gate,
    keyp,
    valp,
    stream,
    decay,
    residue,
    gain,
    query,
    key,
    grad,
    att_o,
    gate_o,
    keyp_o,
    valp_o,
    stream_o,
    gain_o,
    query_o,
    key_o,
    xs,
    conv,
    fac,
    res,
    d64,
    up,
    down,
    ends,
    state_out,
    state_in,
    ein,
    tp_out,
    tp_in,
    gain_out,
    gain_in,
    normed,
    inv,
    dsum,
    swap,
    big,
    exps,
    work,
    dprob,
    rel,
    ml,
    dl,
    fs,
    dos,
    qs,
    ls,
    lcol,
    ret_out,
    ret_in,
    st_s,
    st_r,
    tp_s,
    tp_r,
    ga_s,
    ga_r,
    sw_s,
    sw_r,
    bg_s,
    bg_r,
    ml_s,
    ml_r,
    dl_s,
    dl_r,
    ls_s,
    ls_r,
    rt_s,
    rt_r,
):
    b = lax.axis_index("ctx")
    tp = lax.axis_index("tp")
    x = b // 4
    y = (b // 2) % 2
    a = b % 2
    mine = b % 4
    sibling = b + 1 - 2 * a
    across = b + 2 - 4 * y
    scale = HD**-0.5

    barrier = pltpu.get_barrier_semaphore()

    def greet_ctx(r):
        pl.semaphore_signal(
            barrier, 1, device_id={"ctx": lax.rem(b + r, n_ctx)}, device_id_type=pl.DeviceIdType.MESH
        )

    def greet_tp(r):
        pl.semaphore_signal(
            barrier, 1, device_id={"tp": lax.rem(tp + r, n_tp)}, device_id_type=pl.DeviceIdType.MESH
        )

    loop(1, n_ctx, greet_ctx)
    loop(1, n_tp, greet_tp)

    chunk_id = lax.broadcasted_iota(jnp.int32, (8, HD), 0) % 4
    chunk_f = chunk_id.astype(F32)
    for m in range(MODES):
        rate = halves(decay[m : m + 1, :])
        fac[m] = jnp.exp(-rate)
        res[m] = halves(residue[m : m + 1, :])
        d64[m] = jnp.exp(-CHUNK * rate)
        up[m] = jnp.exp(-CHUNK * rate * chunk_f)
        down[m] = jnp.exp(-CHUNK * rate * (3.0 - chunk_f))
    d256 = jnp.exp(-float(BLK) * decay[...])

    def filter_ends(backward):
        factors = [fac[m] for m in range(MODES)]

        def step(t, states):
            at = CHUNK - 1 - t if backward else t
            column = xs[pl.ds(at, 8, stride=CHUNK), :]
            return tuple(f * s + column for f, s in zip(factors, states))

        zero = jnp.zeros((8, HD), F32)
        states = lax.fori_loop(0, CHUNK, step, (zero,) * MODES, unroll=4)
        weight = up if backward else down
        for m in range(MODES):
            ends[m] = states[m]
            part = states[m] * weight[m]
            ein[m : m + 1, 0:HD] = jnp.sum(part[0:4], axis=0, keepdims=True)
            ein[m : m + 1, HD : 2 * HD] = jnp.sum(part[4:8], axis=0, keepdims=True)
        state_out[int(backward)] = ein[...].astype(BF16)

    def filter_run(backward):
        factors = [fac[m] for m in range(MODES)]
        weights = [res[m] for m in range(MODES)]
        reach = down if backward else up
        entries = []
        for m in range(MODES):
            end = ends[m]
            total = reach[m] * halves(ein[m : m + 1, :])
            power = jnp.ones((8, HD), F32)
            for back in (1, 2, 3):
                moved = pltpu.roll(end, 8 - back if backward else back, 0)
                ok = chunk_id <= 3 - back if backward else chunk_id >= back
                total = total + power * jnp.where(ok, moved, 0.0)
                power = power * d64[m]
            entries.append(total)

        def step(t, states):
            at = CHUNK - 1 - t if backward else t
            column = xs[pl.ds(at, 8, stride=CHUNK), :]
            states = tuple(f * s + column for f, s in zip(factors, states))
            terms = [w * s for w, s in zip(weights, states)]
            while len(terms) > 1:
                terms = [u + v for u, v in zip(terms[::2], terms[1::2])]
            conv[pl.ds(at, 8, stride=CHUNK), :] = terms[0]
            return states

        lax.fori_loop(0, CHUNK, step, tuple(entries), unroll=2)

    def state_copy(way, dst):
        return remote(
            state_out.at[way], state_in.at[way, b], st_s.at[way, dst], st_r.at[way, b], ctx=dst
        )

    def state_wait(way, src):
        remote(
            state_out.at[way], state_in.at[way, src], st_s.at[way, src], st_r.at[way, src], ctx=src
        ).wait_recv()

    mixed = keyp[...].astype(F32) * valp[...].astype(F32)
    xs[0:BLK, :] = mixed[:, :HD]
    xs[BLK:, :] = mixed[:, HD:]
    filter_ends(False)

    def place(t, array):
        big[t, x, y] = array[:, pl.ds(pl.multiple_of(y * HD, HD), HD)]
        swap[t] = array[:, pl.ds(pl.multiple_of((1 - y) * HD, HD), HD)]

    def swap_copy(t):
        return remote(swap.at[t], big.at[t, x, y], sw_s.at[t], sw_r.at[t], ctx=across)

    def swap_wait(t):
        remote(swap.at[t], big.at[t, x, 1 - y], sw_s.at[t], sw_r.at[t], ctx=across).wait_recv()

    def x_copy(t, piece, to):
        return remote(
            big.at[t, x, piece],
            big.at[t, x, piece],
            bg_s.at[t, piece, to],
            bg_r.at[t, piece, x],
            ctx=4 * to + mine,
        )

    def sib_copy(t, piece):
        return remote(
            big.at[t, x, piece],
            big.at[t, 4, piece],
            bg_s.at[t, piece, x],
            bg_r.at[t, piece, 4],
            ctx=sibling,
        )

    def piece_wait(t, piece, slot):
        remote(
            big.at[t, x, piece],
            big.at[t, slot, piece],
            bg_s.at[t, piece, slot % 4],
            bg_r.at[t, piece, slot],
            ctx=sibling,
        ).wait_recv()

    def targets(t, body):
        if t in (Q, DO):
            loop(0, x, lambda i: body(x - 1 - i))
        else:
            loop(x + 1, NX, body)

    def send_piece(t, piece):
        sib_copy(t, piece).start()
        targets(t, lambda to: x_copy(t, piece, to).start())

    def drain_piece(t, piece):
        sib_copy(t, piece).wait_send()
        targets(t, lambda to: x_copy(t, piece, to).wait_send())

    place(Q, query)
    place(DO, grad)
    place(K, key)
    rel[...] = (
        lax.broadcasted_iota(jnp.int32, (BLK, 2 * BLK), 1)
        + BLK * (lax.broadcasted_iota(jnp.int32, (BLK, 2 * BLK), 1) // BLK)
        + BLK * a
        - lax.broadcasted_iota(jnp.int32, (BLK, 2 * BLK), 0)
    )

    pl.semaphore_wait(barrier, n_ctx + n_tp - 2)

    loop(b + 1, n_ctx, lambda dst: state_copy(0, dst).start())
    for t in (Q, DO, K):
        swap_copy(t).start()
    for t in (Q, DO, K):
        send_piece(t, y)
    swap_wait(Q)
    send_piece(Q, 1 - y)

    def gather_states(way):
        def hop(i, total):
            src = n_ctx - 1 - i if way else i
            state_wait(way, src)
            return d256 * total + state_in[way, src].astype(F32)

        count = n_ctx - 1 - b if way else b
        ein[...] = lax.fori_loop(0, count, hop, jnp.zeros((MODES, 2 * HD), F32))

    def tp_copy(which, r):
        return remote(
            tp_out.at[which],
            tp_in.at[which, n_tp - 1 - r],
            tp_s.at[which],
            tp_r.at[which],
            tp=lax.rem(tp + r, n_tp),
        )

    def tp_all(which):
        return remote(
            tp_in.at[which], tp_in.at[which], tp_s.at[which], tp_r.at[which], tp=lax.rem(tp + 1, n_tp)
        )

    gather_states(0)
    filter_run(False)
    total = stream[...].astype(F32) + gate[...].astype(F32) * jnp.concatenate(
        [conv[0:BLK, :], conv[BLK:, :]], axis=1
    )
    normed[...] = total
    tp_out[0] = row_sums(total * total)
    loop(1, n_tp, lambda r: tp_copy(0, r).start())

    for t in (DO, K):
        swap_wait(t)
        send_piece(t, 1 - y)

    def chip_tile(t, r):
        return big[t, jnp.where(r % 2 == a, x, 4), r // 2]

    def x_tile(t, slot):
        return big[t, slot].reshape(2 * BLK, HD)

    neg = jnp.full((4, 2 * BLK), FILL, F32)
    ml[x, 0:4] = neg
    ml[x, 4:8] = jnp.zeros_like(neg)

    def key_scores(xq):
        def tile(r, top):
            s = dot_nt(chip_tile(K, r), x_tile(Q, xq)) * (scale * LOG2E)
            s = jnp.where(rel[...] >= BLK * r - 4 * BLK * (xq - x), s, FILL)
            work[r] = s
            return jnp.maximum(top, jnp.max(s, axis=0, keepdims=True))

        top = lax.fori_loop(0, 4, tile, jnp.full((1, 2 * BLK), FILL, F32))

        def tile_exp(r, total):
            e = jnp.exp2(work[r] - top)
            exps[xq, r] = e.astype(BF16)
            return total + jnp.sum(e, axis=0, keepdims=True)

        total = lax.fori_loop(0, 4, tile_exp, jnp.zeros((1, 2 * BLK), F32))
        ml[x, pl.ds(xq, 1)] = top
        ml[x, pl.ds(4 + xq, 1)] = total

    for piece in (0, 1):
        piece_wait(K, piece, 4)
    key_scores(x)

    def tp_total(which):
        tp_all(which).wait_recv()
        return jnp.sum(tp_in[which], axis=0) + tp_out[which]

    inverse = columns(lax.rsqrt(tp_total(0) / float(n_tp * 2 * HD) + EPS))
    inv[...] = inverse
    normed[...] = normed[...] * jnp.concatenate([inverse, inverse], axis=1)
    swap[V] = jnp.zeros((BLK, HD), BF16)
    vals = (normed[...] * gain[...]).astype(BF16)

    @pl.when(y == 0)
    def _():
        big[V, x, 0] = vals[:, :HD]
        swap[V] = vals[:, HD:]

    @pl.when(y == 1)
    def _():
        big[V, x, 1] = vals[:, HD:]
        swap[V] = vals[:, :HD]

    swap_copy(V).start()
    send_piece(V, y)

    def later_scores(xq):
        for piece in (0, 1):
            piece_wait(Q, piece, xq)
        key_scores(xq)

    loop(x + 1, NX, later_scores)
    swap_wait(V)
    send_piece(V, 1 - y)

    def stat_copy(buf, send, recv, to):
        return remote(buf.at[x], buf.at[x], send.at[to], recv.at[x], ctx=4 * to + mine)

    def stat_wait(buf, send, recv, src):
        remote(buf.at[src], buf.at[src], send.at[src], recv.at[src], ctx=4 * src + mine).wait_recv()

    def others(body):
        loop(1, NX, lambda r: body(lax.rem(x + r, NX)))

    others(lambda to: stat_copy(ml, ml_s, ml_r, to).start())
    others(lambda src: stat_wait(ml, ml_s, ml_r, src))
    tops = jnp.max(ml[:, 0:4, :], axis=0)
    sums = jnp.sum(ml[:, 4:8, :] * jnp.exp2(ml[:, 0:4, :] - tops[None]), axis=0)
    lse = tops + jnp.log2(sums)
    fs[4:8] = lse
    fs[0:4] = jnp.exp2(ml[x, 0:4] - lse)

    def sib_stat(kind):
        return remote(ls.at[kind, 0], ls.at[kind, 1], ls_s.at[kind], ls_r.at[kind], ctx=sibling)

    ls[0, 0] = fs[pl.ds(4 + x, 1)]
    sib_stat(0).start()

    def scale_rows(xq):
        f = columns(fs[pl.ds(xq, 1)])
        dos[xq] = (x_tile(DO, xq).astype(F32) * f).astype(BF16)
        qs[xq] = (x_tile(Q, xq).astype(F32) * (f * scale)).astype(BF16)

    def later_rows(xq):
        for piece in (0, 1):
            piece_wait(DO, piece, xq)
        scale_rows(xq)

    scale_rows(x)
    loop(x + 1, NX, later_rows)

    def ret_copy(t, r):
        return remote(
            ret_out.at[t, r], ret_in.at[t, mine], rt_s.at[t, r], rt_r.at[t, mine], ctx=4 * x + r
        )

    def ret_wait(t, src):
        remote(
            ret_out.at[t, src], ret_in.at[t, src], rt_s.at[t, src], rt_r.at[t, src], ctx=4 * x + src
        ).wait_recv()

    def quad(body):
        loop(1, 4, lambda i: body(lax.rem(mine + i, 4)))

    def give_back(t, r, value):
        ret_out[t, r] = value.astype(BF16)

        @pl.when(r != mine)
        def _():
            ret_copy(t, r).start()

        @pl.when(r == mine)
        def _():
            ret_in[t, mine] = ret_out[t, mine]

    def take_back(t):
        quad(lambda src: ret_wait(t, src))
        return jnp.concatenate(
            [
                ret_in[t, 0].astype(F32) + ret_in[t, 1].astype(F32),
                ret_in[t, 2].astype(F32) + ret_in[t, 3].astype(F32),
            ],
            axis=1,
        )

    zero_tile = jnp.zeros((BLK, HD), F32)

    def value_grads(r):
        total = lax.fori_loop(
            x, NX, lambda xq, acc: acc + dot(exps[xq, r], dos[xq]), zero_tile
        )
        give_back(R_DV, r, total)

    loop(0, 4, value_grads)

    for piece in (0, 1):
        piece_wait(V, piece, 4)
    dl[x] = jnp.zeros((8, 2 * BLK), F32)

    def key_delta(xq):
        def tile(r, total):
            dp = dot_nt(chip_tile(V, r), x_tile(DO, xq))
            dprob[xq, r] = dp
            return total + jnp.sum(exps[xq, r].astype(F32) * dp, axis=0, keepdims=True)

        total = lax.fori_loop(0, 4, tile, jnp.zeros((1, 2 * BLK), F32))
        dl[x, pl.ds(xq, 1)] = total * fs[pl.ds(xq, 1)]

    loop(x, NX, key_delta)
    others(lambda to: stat_copy(dl, dl_s, dl_r, to).start())

    dvalues = take_back(R_DV)
    dsum[...] = dvalues * gain[...]
    tp_out[1] = row_sums(dsum[...] * normed[...])
    loop(1, n_tp, lambda r: tp_copy(1, r).start())
    gain_out[...] = jnp.sum(dvalues * normed[...], axis=0, keepdims=True)

    def gain_copy(r):
        return remote(
            gain_out, gain_in.at[n_ctx - 1 - r], ga_s.at[0], ga_r.at[0], ctx=lax.rem(b + r, n_ctx)
        )

    loop(1, n_ctx, lambda r: gain_copy(r).start())

    others(lambda src: stat_wait(dl, dl_s, dl_r, src))
    fs[0:8] = jnp.sum(dl[...], axis=0)
    ls[1, 0] = fs[pl.ds(x, 1)]
    sib_stat(1).start()

    dot_col = columns(tp_total(1) / float(n_tp * 2 * HD))
    inverse2 = jnp.concatenate([inv[...], inv[...]], axis=1)
    dsummed = inverse2 * (dsum[...] - normed[...] * jnp.concatenate([dot_col, dot_col], axis=1))
    stream_o[...] = dsummed.astype(BF16)
    gate_o[...] = (
        dsummed * jnp.concatenate([conv[0:BLK, :], conv[BLK:, :]], axis=1)
    ).astype(BF16)
    back = dsummed * gate[...].astype(F32)
    xs[0:BLK, :] = back[:, :HD]
    xs[BLK:, :] = back[:, HD:]
    filter_ends(True)
    loop(0, b, lambda dst: state_copy(1, dst).start())

    def key_grads(r):
        def add(xq, acc):
            ds = exps[xq, r].astype(F32) * (dprob[xq, r] - fs[pl.ds(xq, 1)])
            return acc + dot(ds.astype(BF16), qs[xq])

        give_back(R_DK, r, lax.fori_loop(x, NX, add, zero_tile))

    loop(0, 4, key_grads)

    gather_states(1)
    filter_run(True)
    dmixed = jnp.concatenate([conv[0:BLK, :], conv[BLK:, :]], axis=1)
    keyp_o[...] = (dmixed * valp[...].astype(F32)).astype(BF16)
    valp_o[...] = (dmixed * keyp[...].astype(F32)).astype(BF16)

    for kind in (0, 1):
        sib_stat(kind).wait_recv()
        for who in (0, 1):
            lcol[kind, who] = columns(ls[kind, who]).reshape(2, BLK, HD)
    for t in (Q, DO):
        for piece in (0, 1):
            piece_wait(t, piece, 4)

    def earlier_wait(src):
        for t in (K, V):
            for piece in (0, 1):
                piece_wait(t, piece, src)

    loop(0, x, earlier_wait)

    def wide(col):
        return jnp.concatenate([col] * 4, axis=1)

    def query_rows(r):
        who = jnp.where(r % 2 == a, 0, 1)

        def add(xk, acc):
            att, dq = acc
            s = dot_nt(chip_tile(Q, r), x_tile(K, xk)) * (scale * LOG2E)
            p = jnp.exp2(s - wide(lcol[0, who, r // 2]))
            p = jnp.where(rel[...] <= BLK * r + 4 * BLK * (x - xk), p, 0.0)
            dp = dot_nt(chip_tile(DO, r), x_tile(V, xk))
            ds = p * (dp - wide(lcol[1, who, r // 2]))
            return (
                att + dot(p.astype(BF16), x_tile(V, xk)),
                dq + dot(ds.astype(BF16), x_tile(K, xk)),
            )

        att, dq = lax.fori_loop(0, x + 1, add, (zero_tile, zero_tile))
        give_back(R_ATT, r, att)
        give_back(R_DQ, r, dq * scale)

    loop(0, 4, query_rows)

    remote(gain_in, gain_in, ga_s.at[0], ga_r.at[0], ctx=sibling).wait_recv()
    gain_o[...] = jnp.sum(gain_in[...], axis=0) + gain_out[...]
    key_o[...] = take_back(R_DK).astype(BF16)
    att_o[...] = take_back(R_ATT).astype(BF16)
    query_o[...] = take_back(R_DQ).astype(BF16)

    loop(b + 1, n_ctx, lambda dst: state_copy(0, dst).wait_send())
    loop(0, b, lambda dst: state_copy(1, dst).wait_send())
    for t in (Q, DO, K, V):
        swap_copy(t).wait_send()
        for piece in (0, 1):
            drain_piece(t, piece)
    for which in (0, 1):
        tp_all(which).wait_send()
        sib_stat(which).wait_send()
    remote(gain_in, gain_in, ga_s.at[0], ga_r.at[0], ctx=sibling).wait_send()
    others(lambda to: stat_copy(ml, ml_s, ml_r, to).wait_send())
    others(lambda to: stat_copy(dl, dl_s, dl_r, to).wait_send())
    for t in (R_DV, R_DK, R_ATT, R_DQ):
        quad(lambda r: ret_copy(t, r).wait_send())


def on_device(n_ctx, n_tp, *arrays):
    (gate, keyp, valp, stream, decay, residue, gain, query, key, grad) = arrays
    rows, chans = stream.shape
    vmem = pl.BlockSpec(memory_space=pltpu.VMEM)
    full = jax.ShapeDtypeStruct((rows, chans), BF16)
    dma = pltpu.SemaphoreType.DMA

    def body(*refs):
        kernel(n_ctx, n_tp, *refs)

    scratch = [
        pltpu.VMEM((2 * BLK, HD), F32),
        pltpu.VMEM((2 * BLK, HD), F32),
        *[pltpu.VMEM((MODES, 8, HD), F32)] * 6,
        pltpu.VMEM((2, MODES, 2 * HD), BF16),
        pltpu.VMEM((2, n_ctx, MODES, 2 * HD), BF16),
        pltpu.VMEM((MODES, 2 * HD), F32),
        pltpu.VMEM((2, 1, BLK), F32),
        pltpu.VMEM((2, n_tp - 1, 1, BLK), F32),
        pltpu.VMEM((1, 2 * HD), F32),
        pltpu.VMEM((n_ctx - 1, 1, 2 * HD), F32),
        pltpu.VMEM((BLK, 2 * HD), F32),
        pltpu.VMEM((BLK, HD), F32),
        pltpu.VMEM((BLK, 2 * HD), F32),
        pltpu.VMEM((4, BLK, HD), BF16),
        pltpu.VMEM((4, 5, 2, BLK, HD), BF16),
        pltpu.VMEM((NX, 4, BLK, 2 * BLK), BF16),
        pltpu.VMEM((4, BLK, 2 * BLK), F32),
        pltpu.VMEM((NX, 4, BLK, 2 * BLK), F32),
        pltpu.VMEM((BLK, 2 * BLK), jnp.int32),
        pltpu.VMEM((NX, 8, 2 * BLK), F32),
        pltpu.VMEM((NX, 8, 2 * BLK), F32),
        pltpu.VMEM((8, 2 * BLK), F32),
        pltpu.VMEM((NX, 2 * BLK, HD), BF16),
        pltpu.VMEM((NX, 2 * BLK, HD), BF16),
        pltpu.VMEM((2, 2, 1, 2 * BLK), F32),
        pltpu.VMEM((2, 2, 2, BLK, HD), F32),
        pltpu.VMEM((4, 4, BLK, HD), BF16),
        pltpu.VMEM((4, 4, BLK, HD), BF16),
        dma((2, n_ctx)),
        dma((2, n_ctx)),
        dma((2,)),
        dma((2,)),
        dma((1,)),
        dma((1,)),
        dma((4,)),
        dma((4,)),
        dma((4, 2, 4)),
        dma((4, 2, 5)),
        dma((NX,)),
        dma((NX,)),
        dma((NX,)),
        dma((NX,)),
        dma((2,)),
        dma((2,)),
        dma((4, 4)),
        dma((4, 4)),
    ]
    outs = pl.pallas_call(
        body,
        out_shape=(full,) * 5 + (jax.ShapeDtypeStruct((1, chans), F32),) + (full,) * 2,
        in_specs=[vmem] * 10,
        out_specs=(vmem,) * 8,
        scratch_shapes=scratch,
        compiler_params=pltpu.CompilerParams(
            collective_id=0, has_side_effects=True, vmem_limit_bytes=48 * 1024 * 1024
        ),
    )(gate, keyp, valp, stream, decay, residue, gain.reshape(1, chans), query, key, grad)
    return outs[:5] + (outs[5].reshape(chans),) + outs[6:]


def solution(mesh):
    n_ctx, n_tp = mesh.shape["ctx"], mesh.shape["tp"]
    both = P("ctx", "tp")

    def body(*arrays):
        return on_device(n_ctx, n_tp, *arrays)

    return jax.shard_map(
        body,
        mesh=mesh,
        in_specs=(both,) * 4 + (P(None, "tp"), P(None, "tp"), P("tp")) + (both,) * 3,
        out_specs=(both,) * 5 + (P("tp"),) + (both,) * 2,
        check_vma=False,
    )
```

```python
import jax
import jax.numpy as jnp
from jax import lax
from jax.experimental import pallas as pl
from jax.experimental.pallas import tpu as pltpu
from jax.sharding import PartitionSpec as P

HD = 128
BLK = 256
MODES = 16
CHUNK = 64
NX = 4
FILL = -1e30
VMEM = 63 * 1024 * 1024
EPS = 1e-06
LOG2E = 1.4426950408889634
NT = (((1,), (1,)), ((), ()))
HIGHEST = lax.Precision.HIGHEST
F32 = jnp.float32
BF16 = jnp.bfloat16
Q, DO, K, V = 0, 1, 2, 3
R_DV, R_DK, R_ATT, R_DQ = 0, 1, 2, 3


def remote(src, dst, send, recv, **where):
    return pltpu.make_async_remote_copy(
        src_ref=src,
        dst_ref=dst,
        send_sem=send,
        recv_sem=recv,
        device_id=where,
        device_id_type=pl.DeviceIdType.MESH,
    )


def loop(lo, hi, body):
    def step(i, carry):
        body(i)
        return carry

    lax.fori_loop(lo, hi, step, 0)


def halves(row):
    return jnp.concatenate(
        [jnp.broadcast_to(row[:, :HD], (4, HD)), jnp.broadcast_to(row[:, HD:], (4, HD))], axis=0
    )


def columns(row):
    return jnp.transpose(jnp.broadcast_to(row, (HD, row.shape[1])))


def row_sums(x):
    ones = jnp.ones((8, x.shape[1]), F32)
    return lax.dot_general(ones, x, NT, precision=HIGHEST, preferred_element_type=F32)[0:1]


def dot_nt(a, b):
    return lax.dot_general(a, b, NT, preferred_element_type=F32)


def dot(a, b):
    return jnp.dot(a, b, preferred_element_type=F32)


def kernel(
    n_ctx,
    n_tp,
    gate_h,
    keyp_h,
    valp_h,
    stream_h,
    decay_h,
    residue_h,
    gain_h,
    query_h,
    key_h,
    grad_h,
    att_h,
    gateg_h,
    keypg_h,
    valpg_h,
    streamg_h,
    gaing_h,
    queryg_h,
    keyg_h,
    gate,
    keyp,
    valp,
    stream,
    decay,
    residue,
    gain,
    query,
    key,
    grad,
    att_o,
    gate_o,
    keyp_o,
    valp_o,
    stream_o,
    gain_o,
    query_o,
    key_o,
    xs,
    conv,
    fac,
    res,
    d64,
    up,
    down,
    ends,
    state_out,
    state_in,
    ein,
    tp_out,
    tp_in,
    gain_out,
    gain_in,
    normed,
    inv,
    dsum,
    swap,
    big,
    exps,
    work,
    dprob,
    rel,
    ml,
    dl,
    fs,
    dos,
    qs,
    ls,
    lcol,
    ret_out,
    ret_in,
    st_s,
    st_r,
    tp_s,
    tp_r,
    ga_s,
    ga_r,
    sw_s,
    sw_r,
    bg_s,
    bg_r,
    ml_s,
    ml_r,
    dl_s,
    dl_r,
    ls_s,
    ls_r,
    rt_s,
    rt_r,
    in_s,
    out_s,
):
    b = lax.axis_index("ctx")
    tp = lax.axis_index("tp")
    x = b // 4
    y = (b // 2) % 2
    a = b % 2
    mine = b % 4
    sibling = b + 1 - 2 * a
    across = b + 2 - 4 * y
    scale = HD**-0.5

    loads = [
        pltpu.make_async_copy(src, dst, in_s.at[i])
        for i, (src, dst) in enumerate(
            (
                (decay_h, decay),
                (residue_h, residue),
                (keyp_h, keyp),
                (valp_h, valp),
                (query_h, query),
                (grad_h, grad),
                (key_h, key),
                (gate_h, gate),
                (stream_h, stream),
                (gain_h, gain),
            )
        )
    ]
    for load in loads:
        load.start()

    results = (
        (att_o, att_h),
        (gate_o, gateg_h),
        (keyp_o, keypg_h),
        (valp_o, valpg_h),
        (stream_o, streamg_h),
        (gain_o, gaing_h),
        (query_o, queryg_h),
        (key_o, keyg_h),
    )
    stores = [pltpu.make_async_copy(v, h, out_s.at[i]) for i, (v, h) in enumerate(results)]

    barrier = pltpu.get_barrier_semaphore()

    def greet_ctx(r):
        pl.semaphore_signal(
            barrier, 1, device_id={"ctx": lax.rem(b + r, n_ctx)}, device_id_type=pl.DeviceIdType.MESH
        )

    def greet_tp(r):
        pl.semaphore_signal(
            barrier, 1, device_id={"tp": lax.rem(tp + r, n_tp)}, device_id_type=pl.DeviceIdType.MESH
        )

    loop(1, n_ctx, greet_ctx)
    loop(1, n_tp, greet_tp)

    for load in loads[:2]:
        load.wait()
    chunk_id = lax.broadcasted_iota(jnp.int32, (8, HD), 0) % 4
    chunk_f = chunk_id.astype(F32)
    for m in range(MODES):
        rate = halves(decay[m : m + 1, :])
        fac[m] = jnp.exp(-rate)
        res[m] = halves(residue[m : m + 1, :])
        d64[m] = jnp.exp(-CHUNK * rate)
        up[m] = jnp.exp(-CHUNK * rate * chunk_f)
        down[m] = jnp.exp(-CHUNK * rate * (3.0 - chunk_f))
    d256 = jnp.exp(-float(BLK) * decay[...])

    def filter_ends(backward):
        factors = [fac[m] for m in range(MODES)]

        def step(t, states):
            at = CHUNK - 1 - t if backward else t
            column = xs[pl.ds(at, 8, stride=CHUNK), :]
            return tuple(f * s + column for f, s in zip(factors, states))

        zero = jnp.zeros((8, HD), F32)
        states = lax.fori_loop(0, CHUNK, step, (zero,) * MODES, unroll=4)
        weight = up if backward else down
        for m in range(MODES):
            ends[m] = states[m]
            part = states[m] * weight[m]
            ein[m : m + 1, 0:HD] = jnp.sum(part[0:4], axis=0, keepdims=True)
            ein[m : m + 1, HD : 2 * HD] = jnp.sum(part[4:8], axis=0, keepdims=True)
        state_out[int(backward)] = ein[...].astype(BF16)

    def filter_run(backward):
        factors = [fac[m] for m in range(MODES)]
        weights = [res[m] for m in range(MODES)]
        reach = down if backward else up
        entries = []
        for m in range(MODES):
            end = ends[m]
            total = reach[m] * halves(ein[m : m + 1, :])
            power = jnp.ones((8, HD), F32)
            for back in (1, 2, 3):
                moved = pltpu.roll(end, 8 - back if backward else back, 0)
                ok = chunk_id <= 3 - back if backward else chunk_id >= back
                total = total + power * jnp.where(ok, moved, 0.0)
                power = power * d64[m]
            entries.append(total)

        def step(t, states):
            at = CHUNK - 1 - t if backward else t
            column = xs[pl.ds(at, 8, stride=CHUNK), :]
            states = tuple(f * s + column for f, s in zip(factors, states))
            terms = [w * s for w, s in zip(weights, states)]
            while len(terms) > 1:
                terms = [u + v for u, v in zip(terms[::2], terms[1::2])]
            conv[pl.ds(at, 8, stride=CHUNK), :] = terms[0]
            return states

        lax.fori_loop(0, CHUNK, step, tuple(entries), unroll=2)

    def state_copy(way, dst):
        return remote(
            state_out.at[way], state_in.at[way, b], st_s.at[way, dst], st_r.at[way, b], ctx=dst
        )

    def state_wait(way, src):
        remote(
            state_out.at[way], state_in.at[way, src], st_s.at[way, src], st_r.at[way, src], ctx=src
        ).wait_recv()

    for load in loads[2:4]:
        load.wait()
    mixed = keyp[...].astype(F32) * valp[...].astype(F32)
    xs[0:BLK, :] = mixed[:, :HD]
    xs[BLK:, :] = mixed[:, HD:]
    filter_ends(False)

    def place(t, array):
        big[t, x, y] = array[:, pl.ds(pl.multiple_of(y * HD, HD), HD)]
        swap[t] = array[:, pl.ds(pl.multiple_of((1 - y) * HD, HD), HD)]

    def swap_copy(t):
        return remote(swap.at[t], big.at[t, x, y], sw_s.at[t], sw_r.at[t], ctx=across)

    def swap_wait(t):
        remote(swap.at[t], big.at[t, x, 1 - y], sw_s.at[t], sw_r.at[t], ctx=across).wait_recv()

    def x_copy(t, piece, to):
        return remote(
            big.at[t, x, piece],
            big.at[t, x, piece],
            bg_s.at[t, piece, to],
            bg_r.at[t, piece, x],
            ctx=4 * to + mine,
        )

    def sib_copy(t, piece):
        return remote(
            big.at[t, x, piece],
            big.at[t, 4, piece],
            bg_s.at[t, piece, x],
            bg_r.at[t, piece, 4],
            ctx=sibling,
        )

    def piece_wait(t, piece, slot):
        remote(
            big.at[t, x, piece],
            big.at[t, slot, piece],
            bg_s.at[t, piece, slot % 4],
            bg_r.at[t, piece, slot],
            ctx=sibling,
        ).wait_recv()

    def targets(t, body):
        if t in (Q, DO):
            loop(0, x, lambda i: body(x - 1 - i))
        else:
            loop(x + 1, NX, body)

    def send_piece(t, piece):
        sib_copy(t, piece).start()
        targets(t, lambda to: x_copy(t, piece, to).start())

    def drain_piece(t, piece):
        sib_copy(t, piece).wait_send()
        targets(t, lambda to: x_copy(t, piece, to).wait_send())

    for load in loads[4:7]:
        load.wait()
    place(Q, query)
    place(DO, grad)
    place(K, key)
    rel[...] = (
        lax.broadcasted_iota(jnp.int32, (BLK, 2 * BLK), 1)
        + BLK * (lax.broadcasted_iota(jnp.int32, (BLK, 2 * BLK), 1) // BLK)
        + BLK * a
        - lax.broadcasted_iota(jnp.int32, (BLK, 2 * BLK), 0)
    )

    pl.semaphore_wait(barrier, n_ctx + n_tp - 2)

    loop(b + 1, n_ctx, lambda dst: state_copy(0, dst).start())
    for t in (Q, K, DO):
        swap_copy(t).start()
    for t in (Q, K, DO):
        send_piece(t, y)
    for t in (Q, K, DO):
        swap_wait(t)
        send_piece(t, 1 - y)

    def gather_states(way):
        def hop(i, total):
            src = n_ctx - 1 - i if way else i
            state_wait(way, src)
            return d256 * total + state_in[way, src].astype(F32)

        count = n_ctx - 1 - b if way else b
        ein[...] = lax.fori_loop(0, count, hop, jnp.zeros((MODES, 2 * HD), F32))

    def tp_copy(which, r):
        return remote(
            tp_out.at[which],
            tp_in.at[which, n_tp - 1 - r],
            tp_s.at[which],
            tp_r.at[which],
            tp=lax.rem(tp + r, n_tp),
        )

    def tp_all(which):
        return remote(
            tp_in.at[which], tp_in.at[which], tp_s.at[which], tp_r.at[which], tp=lax.rem(tp + 1, n_tp)
        )

    for load in loads[7:]:
        load.wait()
    gather_states(0)
    filter_run(False)
    total = stream[...].astype(F32) + gate[...].astype(F32) * jnp.concatenate(
        [conv[0:BLK, :], conv[BLK:, :]], axis=1
    )
    normed[...] = total
    tp_out[0] = row_sums(total * total)
    loop(1, n_tp, lambda r: tp_copy(0, r).start())

    def chip_tile(t, r):
        return big[t, jnp.where(r % 2 == a, x, 4), r // 2]

    def x_tile(t, slot):
        return big[t, slot].reshape(2 * BLK, HD)

    neg = jnp.full((4, 2 * BLK), FILL, F32)
    ml[x, 0:4] = neg
    ml[x, 4:8] = jnp.zeros_like(neg)

    def key_scores(xq):
        def tile(r, top):
            s = dot_nt(chip_tile(K, r), x_tile(Q, xq)) * (scale * LOG2E)
            s = jnp.where(rel[...] >= BLK * r - 4 * BLK * (xq - x), s, FILL)
            work[r] = s
            return jnp.maximum(top, jnp.max(s, axis=0, keepdims=True))

        top = lax.fori_loop(0, 4, tile, jnp.full((1, 2 * BLK), FILL, F32))

        def tile_exp(r, total):
            e = jnp.exp2(work[r] - top)
            exps[xq, r] = e.astype(BF16)
            return total + jnp.sum(e, axis=0, keepdims=True)

        total = lax.fori_loop(0, 4, tile_exp, jnp.zeros((1, 2 * BLK), F32))
        ml[x, pl.ds(xq, 1)] = top
        ml[x, pl.ds(4 + xq, 1)] = total

    for piece in (0, 1):
        piece_wait(K, piece, 4)
    key_scores(x)

    def later_scores(xq):
        for piece in (0, 1):
            piece_wait(Q, piece, xq)
        key_scores(xq)

    loop(x + 1, NX, later_scores)

    def stat_copy(buf, send, recv, to):
        return remote(buf.at[x], buf.at[x], send.at[to], recv.at[x], ctx=4 * to + mine)

    def stat_wait(buf, send, recv, src):
        remote(buf.at[src], buf.at[src], send.at[src], recv.at[src], ctx=4 * src + mine).wait_recv()

    def others(body):
        loop(1, NX, lambda r: body(lax.rem(x + r, NX)))

    others(lambda to: stat_copy(ml, ml_s, ml_r, to).start())

    def tp_total(which):
        tp_all(which).wait_recv()
        return jnp.sum(tp_in[which], axis=0) + tp_out[which]

    inverse = columns(lax.rsqrt(tp_total(0) / float(n_tp * 2 * HD) + EPS))
    inv[...] = inverse
    normed[...] = normed[...] * jnp.concatenate([inverse, inverse], axis=1)
    swap[V] = jnp.zeros((BLK, HD), BF16)
    vals = (normed[...] * gain[...]).astype(BF16)

    @pl.when(y == 0)
    def _():
        big[V, x, 0] = vals[:, :HD]
        swap[V] = vals[:, HD:]

    @pl.when(y == 1)
    def _():
        big[V, x, 1] = vals[:, HD:]
        swap[V] = vals[:, :HD]

    swap_copy(V).start()
    send_piece(V, y)

    others(lambda src: stat_wait(ml, ml_s, ml_r, src))
    tops = jnp.max(ml[:, 0:4, :], axis=0)
    sums = jnp.sum(ml[:, 4:8, :] * jnp.exp2(ml[:, 0:4, :] - tops[None]), axis=0)
    lse = tops + jnp.log2(sums)
    fs[4:8] = lse
    fs[0:4] = jnp.exp2(ml[x, 0:4] - lse)

    def sib_stat(kind):
        return remote(ls.at[kind, 0], ls.at[kind, 1], ls_s.at[kind], ls_r.at[kind], ctx=sibling)

    ls[0, 0] = fs[pl.ds(4 + x, 1)]
    sib_stat(0).start()

    def scale_rows(xq):
        f = columns(fs[pl.ds(xq, 1)])
        dos[xq] = (x_tile(DO, xq).astype(F32) * f).astype(BF16)
        qs[xq] = (x_tile(Q, xq).astype(F32) * (f * scale)).astype(BF16)

    def later_rows(xq):
        for piece in (0, 1):
            piece_wait(DO, piece, xq)
        scale_rows(xq)

    scale_rows(x)
    loop(x + 1, NX, later_rows)

    def ret_copy(t, r):
        return remote(
            ret_out.at[t, r], ret_in.at[t, mine], rt_s.at[t, r], rt_r.at[t, mine], ctx=4 * x + r
        )

    def ret_wait(t, src):
        remote(
            ret_out.at[t, src], ret_in.at[t, src], rt_s.at[t, src], rt_r.at[t, src], ctx=4 * x + src
        ).wait_recv()

    def quad(body):
        loop(1, 4, lambda i: body(lax.rem(mine + i, 4)))

    def give_back(t, r, value):
        ret_out[t, r] = value.astype(BF16)

        @pl.when(r != mine)
        def _():
            ret_copy(t, r).start()

        @pl.when(r == mine)
        def _():
            ret_in[t, mine] = ret_out[t, mine]

    def take_back(t):
        quad(lambda src: ret_wait(t, src))
        return jnp.concatenate(
            [
                ret_in[t, 0].astype(F32) + ret_in[t, 1].astype(F32),
                ret_in[t, 2].astype(F32) + ret_in[t, 3].astype(F32),
            ],
            axis=1,
        )

    zero_tile = jnp.zeros((BLK, HD), F32)

    def value_grads(r):
        total = lax.fori_loop(
            x, NX, lambda xq, acc: acc + dot(exps[xq, r], dos[xq]), zero_tile
        )
        give_back(R_DV, r, total)

    loop(0, 4, value_grads)

    swap_wait(V)
    send_piece(V, 1 - y)
    for piece in (0, 1):
        piece_wait(V, piece, 4)
    dl[x] = jnp.zeros((8, 2 * BLK), F32)

    def key_delta(xq):
        def tile(r, total):
            dp = dot_nt(chip_tile(V, r), x_tile(DO, xq))
            dprob[xq, r] = dp
            return total + jnp.sum(exps[xq, r].astype(F32) * dp, axis=0, keepdims=True)

        total = lax.fori_loop(0, 4, tile, jnp.zeros((1, 2 * BLK), F32))
        dl[x, pl.ds(xq, 1)] = total * fs[pl.ds(xq, 1)]

    loop(x, NX, key_delta)
    others(lambda to: stat_copy(dl, dl_s, dl_r, to).start())

    dvalues = take_back(R_DV)
    dsum[...] = dvalues * gain[...]
    tp_out[1] = row_sums(dsum[...] * normed[...])
    loop(1, n_tp, lambda r: tp_copy(1, r).start())
    gain_out[...] = jnp.sum(dvalues * normed[...], axis=0, keepdims=True)

    def gain_copy(r):
        return remote(
            gain_out, gain_in.at[n_ctx - 1 - r], ga_s.at[0], ga_r.at[0], ctx=lax.rem(b + r, n_ctx)
        )

    loop(1, n_ctx, lambda r: gain_copy(r).start())

    others(lambda src: stat_wait(dl, dl_s, dl_r, src))
    fs[0:8] = jnp.sum(dl[...], axis=0)
    ls[1, 0] = fs[pl.ds(x, 1)]
    sib_stat(1).start()

    def key_grads(r):
        def add(xq, acc):
            ds = exps[xq, r].astype(F32) * (dprob[xq, r] - fs[pl.ds(xq, 1)])
            return acc + dot(ds.astype(BF16), qs[xq])

        give_back(R_DK, r, lax.fori_loop(x, NX, add, zero_tile))

    loop(0, 4, key_grads)

    for kind in (0, 1):
        sib_stat(kind).wait_recv()
        for who in (0, 1):
            lcol[kind, who] = columns(ls[kind, who]).reshape(2, BLK, HD)
    for t in (Q, DO):
        for piece in (0, 1):
            piece_wait(t, piece, 4)

    def earlier_wait(src):
        for t in (K, V):
            for piece in (0, 1):
                piece_wait(t, piece, src)

    loop(0, x, earlier_wait)

    def wide(col):
        return jnp.concatenate([col] * 4, axis=1)

    def query_rows(r):
        who = jnp.where(r % 2 == a, 0, 1)

        def add(xk, acc):
            att, dq = acc
            s = dot_nt(chip_tile(Q, r), x_tile(K, xk)) * (scale * LOG2E)
            p = jnp.exp2(s - wide(lcol[0, who, r // 2]))
            p = jnp.where(rel[...] <= BLK * r + 4 * BLK * (x - xk), p, 0.0)
            dp = dot_nt(chip_tile(DO, r), x_tile(V, xk))
            ds = p * (dp - wide(lcol[1, who, r // 2]))
            return (
                att + dot(p.astype(BF16), x_tile(V, xk)),
                dq + dot(ds.astype(BF16), x_tile(K, xk)),
            )

        att, dq = lax.fori_loop(0, x + 1, add, (zero_tile, zero_tile))
        give_back(R_ATT, r, att)
        give_back(R_DQ, r, dq * scale)

    loop(0, 4, query_rows)

    dot_col = columns(tp_total(1) / float(n_tp * 2 * HD))
    inverse2 = jnp.concatenate([inv[...], inv[...]], axis=1)
    dsummed = inverse2 * (dsum[...] - normed[...] * jnp.concatenate([dot_col, dot_col], axis=1))
    stream_o[...] = dsummed.astype(BF16)
    gate_o[...] = (
        dsummed * jnp.concatenate([conv[0:BLK, :], conv[BLK:, :]], axis=1)
    ).astype(BF16)
    stores[4].start()
    stores[1].start()
    back = dsummed * gate[...].astype(F32)
    xs[0:BLK, :] = back[:, :HD]
    xs[BLK:, :] = back[:, HD:]
    filter_ends(True)
    loop(0, b, lambda dst: state_copy(1, dst).start())

    remote(gain_in, gain_in, ga_s.at[0], ga_r.at[0], ctx=sibling).wait_recv()
    gain_o[...] = jnp.sum(gain_in[...], axis=0) + gain_out[...]
    stores[5].start()
    key_o[...] = take_back(R_DK).astype(BF16)
    stores[7].start()
    att_o[...] = take_back(R_ATT).astype(BF16)
    stores[0].start()
    query_o[...] = take_back(R_DQ).astype(BF16)
    stores[6].start()

    gather_states(1)
    filter_run(True)
    dmixed = jnp.concatenate([conv[0:BLK, :], conv[BLK:, :]], axis=1)
    keyp_o[...] = (dmixed * valp[...].astype(F32)).astype(BF16)
    valp_o[...] = (dmixed * keyp[...].astype(F32)).astype(BF16)

    stores[2].start()
    stores[3].start()

    loop(b + 1, n_ctx, lambda dst: state_copy(0, dst).wait_send())
    loop(0, b, lambda dst: state_copy(1, dst).wait_send())
    for t in (Q, DO, K, V):
        swap_copy(t).wait_send()
        for piece in (0, 1):
            drain_piece(t, piece)
    for which in (0, 1):
        tp_all(which).wait_send()
        sib_stat(which).wait_send()
    remote(gain_in, gain_in, ga_s.at[0], ga_r.at[0], ctx=sibling).wait_send()
    others(lambda to: stat_copy(ml, ml_s, ml_r, to).wait_send())
    others(lambda to: stat_copy(dl, dl_s, dl_r, to).wait_send())
    for t in (R_DV, R_DK, R_ATT, R_DQ):
        quad(lambda r: ret_copy(t, r).wait_send())
    for copy in stores:
        copy.wait()


def store(*refs):
    held, sem = refs[16:24], refs[24]
    arrive = [pltpu.make_async_copy(refs[i], held[i], sem.at[0, i]) for i in range(8)]
    leave = [pltpu.make_async_copy(held[i], refs[8 + i], sem.at[1, i]) for i in range(8)]
    for copy in arrive:
        copy.start()
    for one, other in zip(arrive, leave):
        one.wait()
        other.start()
    for copy in leave:
        copy.wait()


def on_device(n_ctx, n_tp, *arrays):
    (gate, keyp, valp, stream, decay, residue, gain, query, key, grad) = arrays
    rows, chans = stream.shape
    full = jax.ShapeDtypeStruct((rows, chans), BF16)
    dma = pltpu.SemaphoreType.DMA

    def body(*refs):
        kernel(n_ctx, n_tp, *refs)

    scratch = [
        *[pltpu.VMEM((rows, chans), BF16)] * 4,
        *[pltpu.VMEM((MODES, chans), F32)] * 2,
        pltpu.VMEM((1, chans), F32),
        *[pltpu.VMEM((rows, chans), BF16)] * 3,
        *[pltpu.VMEM((rows, chans), BF16)] * 5,
        pltpu.VMEM((1, chans), F32),
        *[pltpu.VMEM((rows, chans), BF16)] * 2,
        pltpu.VMEM((2 * BLK, HD), F32),
        pltpu.VMEM((2 * BLK, HD), F32),
        *[pltpu.VMEM((MODES, 8, HD), F32)] * 6,
        pltpu.VMEM((2, MODES, 2 * HD), BF16),
        pltpu.VMEM((2, n_ctx, MODES, 2 * HD), BF16),
        pltpu.VMEM((MODES, 2 * HD), F32),
        pltpu.VMEM((2, 1, BLK), F32),
        pltpu.VMEM((2, n_tp - 1, 1, BLK), F32),
        pltpu.VMEM((1, 2 * HD), F32),
        pltpu.VMEM((n_ctx - 1, 1, 2 * HD), F32),
        pltpu.VMEM((BLK, 2 * HD), F32),
        pltpu.VMEM((BLK, HD), F32),
        pltpu.VMEM((BLK, 2 * HD), F32),
        pltpu.VMEM((4, BLK, HD), BF16),
        pltpu.VMEM((4, 5, 2, BLK, HD), BF16),
        pltpu.VMEM((NX, 4, BLK, 2 * BLK), BF16),
        pltpu.VMEM((4, BLK, 2 * BLK), F32),
        pltpu.VMEM((NX, 4, BLK, 2 * BLK), F32),
        pltpu.VMEM((BLK, 2 * BLK), jnp.int32),
        pltpu.VMEM((NX, 8, 2 * BLK), F32),
        pltpu.VMEM((NX, 8, 2 * BLK), F32),
        pltpu.VMEM((8, 2 * BLK), F32),
        pltpu.VMEM((NX, 2 * BLK, HD), BF16),
        pltpu.VMEM((NX, 2 * BLK, HD), BF16),
        pltpu.VMEM((2, 2, 1, 2 * BLK), F32),
        pltpu.VMEM((2, 2, 2, BLK, HD), F32),
        pltpu.VMEM((4, 4, BLK, HD), BF16),
        pltpu.VMEM((4, 4, BLK, HD), BF16),
        dma((2, n_ctx)),
        dma((2, n_ctx)),
        dma((2,)),
        dma((2,)),
        dma((1,)),
        dma((1,)),
        dma((4,)),
        dma((4,)),
        dma((4, 2, 4)),
        dma((4, 2, 5)),
        dma((NX,)),
        dma((NX,)),
        dma((NX,)),
        dma((NX,)),
        dma((2,)),
        dma((2,)),
        dma((4, 4)),
        dma((4, 4)),
        dma((10,)),
        dma((8,)),
    ]
    hbm = pl.BlockSpec(memory_space=pltpu.HBM)
    shapes = (full,) * 5 + (jax.ShapeDtypeStruct((1, chans), F32),) + (full,) * 2
    outs = pl.pallas_call(
        body,
        out_shape=shapes,
        in_specs=[hbm] * 10,
        out_specs=(hbm,) * 8,
        scratch_shapes=scratch,
        compiler_params=pltpu.CompilerParams(
            collective_id=0, has_side_effects=True, vmem_limit_bytes=VMEM
        ),
    )(gate, keyp, valp, stream, decay, residue, gain.reshape(1, chans), query, key, grad)
    outs = pl.pallas_call(
        store,
        out_shape=shapes,
        in_specs=[hbm] * 8,
        out_specs=(hbm,) * 8,
        scratch_shapes=[*[pltpu.VMEM(s.shape, s.dtype) for s in shapes], dma((2, 8))],
        compiler_params=pltpu.CompilerParams(vmem_limit_bytes=VMEM),
    )(*outs)
    return outs[:5] + (outs[5].reshape(chans),) + outs[6:]


def solution(mesh):
    n_ctx, n_tp = mesh.shape["ctx"], mesh.shape["tp"]
    both = P("ctx", "tp")

    def body(*arrays):
        return on_device(n_ctx, n_tp, *arrays)

    return jax.shard_map(
        body,
        mesh=mesh,
        in_specs=(both,) * 4 + (P(None, "tp"), P(None, "tp"), P("tp")) + (both,) * 3,
        out_specs=(both,) * 5 + (P("tp"),) + (both,) * 2,
        check_vma=False,
    )
```

```python
import jax
import jax.numpy as jnp
from jax import lax
from jax.experimental import pallas as pl
from jax.experimental.pallas import tpu as pltpu
from jax.sharding import PartitionSpec as P

HD = 128
BLK = 256
MODES = 16
CHUNK = 64
NX = 4
FILL = -1e30
VMEM = 63 * 1024 * 1024
EPS = 1e-06
LOG2E = 1.4426950408889634
NT = (((1,), (1,)), ((), ()))
HIGHEST = lax.Precision.HIGHEST
F32 = jnp.float32
BF16 = jnp.bfloat16
Q, DO, K, V = 0, 1, 2, 3
R_DV, R_DK, R_ATT, R_DQ = 0, 1, 2, 3


def remote(src, dst, send, recv, **where):
    return pltpu.make_async_remote_copy(
        src_ref=src,
        dst_ref=dst,
        send_sem=send,
        recv_sem=recv,
        device_id=where,
        device_id_type=pl.DeviceIdType.MESH,
    )


def loop(lo, hi, body):
    def step(i, carry):
        body(i)
        return carry

    lax.fori_loop(lo, hi, step, 0)


def halves(row):
    return jnp.concatenate(
        [jnp.broadcast_to(row[:, :HD], (4, HD)), jnp.broadcast_to(row[:, HD:], (4, HD))], axis=0
    )


def columns(row):
    return jnp.transpose(jnp.broadcast_to(row, (HD, row.shape[1])))


def row_sums(x):
    ones = jnp.ones((8, x.shape[1]), F32)
    return lax.dot_general(ones, x, NT, precision=HIGHEST, preferred_element_type=F32)[0:1]


def dot_nt(a, b):
    return lax.dot_general(a, b, NT, preferred_element_type=F32)


def dot(a, b):
    return jnp.dot(a, b, preferred_element_type=F32)


def kernel(
    n_ctx,
    n_tp,
    gate_h,
    keyp_h,
    valp_h,
    stream_h,
    decay_h,
    residue_h,
    gain_h,
    query_h,
    key_h,
    grad_h,
    att_h,
    gateg_h,
    keypg_h,
    valpg_h,
    streamg_h,
    gaing_h,
    queryg_h,
    keyg_h,
    gate,
    keyp,
    valp,
    stream,
    decay,
    residue,
    gain,
    query,
    key,
    grad,
    att_o,
    gate_o,
    keyp_o,
    valp_o,
    stream_o,
    gain_o,
    query_o,
    key_o,
    xs,
    conv,
    fac,
    res,
    d64,
    up,
    down,
    ends,
    state_out,
    state_in,
    ein,
    tp_out,
    tp_in,
    gain_out,
    gain_in,
    normed,
    inv,
    dsum,
    swap,
    big,
    exps,
    work,
    dprob,
    rel,
    ml,
    dl,
    fs,
    acc,
    qs,
    ls,
    lcol,
    ret_out,
    ret_in,
    st_s,
    st_r,
    tp_s,
    tp_r,
    ga_s,
    ga_r,
    sw_s,
    sw_r,
    bg_s,
    bg_r,
    ml_s,
    ml_r,
    dl_s,
    dl_r,
    ls_s,
    ls_r,
    rt_s,
    rt_r,
    in_s,
    out_s,
):
    b = lax.axis_index("ctx")
    tp = lax.axis_index("tp")
    x = b // 4
    y = (b // 2) % 2
    a = b % 2
    mine = b % 4
    sibling = b + 1 - 2 * a
    across = b + 2 - 4 * y
    scale = HD**-0.5

    loads = [
        pltpu.make_async_copy(src, dst, in_s.at[i])
        for i, (src, dst) in enumerate(
            (
                (decay_h, decay),
                (residue_h, residue),
                (keyp_h, keyp),
                (valp_h, valp),
                (query_h, query),
                (grad_h, grad),
                (key_h, key),
                (gate_h, gate),
                (stream_h, stream),
                (gain_h, gain),
            )
        )
    ]
    for load in loads:
        load.start()

    results = (
        (att_o, att_h),
        (gate_o, gateg_h),
        (keyp_o, keypg_h),
        (valp_o, valpg_h),
        (stream_o, streamg_h),
        (gain_o, gaing_h),
        (query_o, queryg_h),
        (key_o, keyg_h),
    )
    stores = [pltpu.make_async_copy(v, h, out_s.at[i]) for i, (v, h) in enumerate(results)]

    barrier = pltpu.get_barrier_semaphore()

    def greet_ctx(r):
        pl.semaphore_signal(
            barrier, 1, device_id={"ctx": lax.rem(b + r, n_ctx)}, device_id_type=pl.DeviceIdType.MESH
        )

    def greet_tp(r):
        pl.semaphore_signal(
            barrier, 1, device_id={"tp": lax.rem(tp + r, n_tp)}, device_id_type=pl.DeviceIdType.MESH
        )

    loop(1, n_ctx, greet_ctx)
    loop(1, n_tp, greet_tp)

    for load in loads[:2]:
        load.wait()
    chunk_id = lax.broadcasted_iota(jnp.int32, (8, HD), 0) % 4
    chunk_f = chunk_id.astype(F32)
    for m in range(MODES):
        rate = halves(decay[m : m + 1, :])
        fac[m] = jnp.exp(-rate)
        res[m] = halves(residue[m : m + 1, :])
        d64[m] = jnp.exp(-CHUNK * rate)
        up[m] = jnp.exp(-CHUNK * rate * chunk_f)
        down[m] = jnp.exp(-CHUNK * rate * (3.0 - chunk_f))
    d256 = jnp.exp(-float(BLK) * decay[...])

    def filter_ends(backward):
        factors = [fac[m] for m in range(MODES)]

        def step(t, states):
            at = CHUNK - 1 - t if backward else t
            column = xs[pl.ds(at, 8, stride=CHUNK), :]
            return tuple(f * s + column for f, s in zip(factors, states))

        zero = jnp.zeros((8, HD), F32)
        states = lax.fori_loop(0, CHUNK, step, (zero,) * MODES, unroll=4)
        weight = up if backward else down
        for m in range(MODES):
            ends[m] = states[m]
            part = states[m] * weight[m]
            ein[m : m + 1, 0:HD] = jnp.sum(part[0:4], axis=0, keepdims=True)
            ein[m : m + 1, HD : 2 * HD] = jnp.sum(part[4:8], axis=0, keepdims=True)
        state_out[int(backward)] = ein[...].astype(BF16)

    def filter_run(backward):
        factors = [fac[m] for m in range(MODES)]
        weights = [res[m] for m in range(MODES)]
        reach = down if backward else up
        entries = []
        for m in range(MODES):
            end = ends[m]
            total = reach[m] * halves(ein[m : m + 1, :])
            power = jnp.ones((8, HD), F32)
            for back in (1, 2, 3):
                moved = pltpu.roll(end, 8 - back if backward else back, 0)
                ok = chunk_id <= 3 - back if backward else chunk_id >= back
                total = total + power * jnp.where(ok, moved, 0.0)
                power = power * d64[m]
            entries.append(total)

        def step(t, states):
            at = CHUNK - 1 - t if backward else t
            column = xs[pl.ds(at, 8, stride=CHUNK), :]
            states = tuple(f * s + column for f, s in zip(factors, states))
            terms = [w * s for w, s in zip(weights, states)]
            while len(terms) > 1:
                terms = [u + v for u, v in zip(terms[::2], terms[1::2])]
            conv[pl.ds(at, 8, stride=CHUNK), :] = terms[0]
            return states

        lax.fori_loop(0, CHUNK, step, tuple(entries), unroll=2)

    def state_copy(way, dst):
        return remote(
            state_out.at[way], state_in.at[way, b], st_s.at[way, dst], st_r.at[way, b], ctx=dst
        )

    def state_wait(way, src):
        remote(
            state_out.at[way], state_in.at[way, src], st_s.at[way, src], st_r.at[way, src], ctx=src
        ).wait_recv()

    for load in loads[2:4]:
        load.wait()
    mixed = keyp[...].astype(F32) * valp[...].astype(F32)
    xs[0:BLK, :] = mixed[:, :HD]
    xs[BLK:, :] = mixed[:, HD:]
    filter_ends(False)

    def place(t, array):
        big[t, x, y] = array[:, pl.ds(pl.multiple_of(y * HD, HD), HD)]
        swap[t] = array[:, pl.ds(pl.multiple_of((1 - y) * HD, HD), HD)]

    def swap_copy(t):
        return remote(swap.at[t], big.at[t, x, y], sw_s.at[t], sw_r.at[t], ctx=across)

    def swap_wait(t):
        remote(swap.at[t], big.at[t, x, 1 - y], sw_s.at[t], sw_r.at[t], ctx=across).wait_recv()

    def x_copy(t, piece, to):
        return remote(
            big.at[t, x, piece],
            big.at[t, x, piece],
            bg_s.at[t, piece, to],
            bg_r.at[t, piece, x],
            ctx=4 * to + mine,
        )

    def sib_copy(t, piece):
        return remote(
            big.at[t, x, piece],
            big.at[t, 4, piece],
            bg_s.at[t, piece, x],
            bg_r.at[t, piece, 4],
            ctx=sibling,
        )

    def piece_wait(t, piece, slot):
        remote(
            big.at[t, x, piece],
            big.at[t, slot, piece],
            bg_s.at[t, piece, slot % 4],
            bg_r.at[t, piece, slot],
            ctx=sibling,
        ).wait_recv()

    def targets(t, body):
        if t in (Q, DO):
            loop(0, x, lambda i: body(x - 1 - i))
        else:
            loop(x + 1, NX, body)

    def send_x(t, piece):
        targets(t, lambda to: x_copy(t, piece, to).start())

    def send_piece(t, piece):
        sib_copy(t, piece).start()
        send_x(t, piece)

    def drain_piece(t, piece):
        sib_copy(t, piece).wait_send()
        targets(t, lambda to: x_copy(t, piece, to).wait_send())

    for load in loads[4:7]:
        load.wait()
    place(Q, query)
    place(DO, grad)
    place(K, key)
    rel[...] = (
        lax.broadcasted_iota(jnp.int32, (BLK, 2 * BLK), 1)
        + BLK * (lax.broadcasted_iota(jnp.int32, (BLK, 2 * BLK), 1) // BLK)
        + BLK * a
        - lax.broadcasted_iota(jnp.int32, (BLK, 2 * BLK), 0)
    )

    pl.semaphore_wait(barrier, n_ctx + n_tp - 2)

    loop(b + 1, n_ctx, lambda dst: state_copy(0, dst).start())
    for t in (Q, K, DO):
        swap_copy(t).start()
    send_x(Q, y)
    sib_copy(K, y).start()
    swap_wait(Q)
    send_x(Q, 1 - y)
    swap_wait(K)
    sib_copy(K, 1 - y).start()
    send_piece(DO, y)
    swap_wait(DO)
    send_piece(DO, 1 - y)
    for piece in (0, 1):
        sib_copy(Q, piece).start()

    def gather_states(way):
        def hop(i, total):
            src = n_ctx - 1 - i if way else i
            state_wait(way, src)
            return d256 * total + state_in[way, src].astype(F32)

        count = n_ctx - 1 - b if way else b
        ein[...] = lax.fori_loop(0, count, hop, jnp.zeros((MODES, 2 * HD), F32))

    def tp_copy(which, r):
        return remote(
            tp_out.at[which],
            tp_in.at[which, n_tp - 1 - r],
            tp_s.at[which],
            tp_r.at[which],
            tp=lax.rem(tp + r, n_tp),
        )

    def tp_all(which):
        return remote(
            tp_in.at[which], tp_in.at[which], tp_s.at[which], tp_r.at[which], tp=lax.rem(tp + 1, n_tp)
        )

    for load in loads[7:]:
        load.wait()
    gather_states(0)
    filter_run(False)
    total = stream[...].astype(F32) + gate[...].astype(F32) * jnp.concatenate(
        [conv[0:BLK, :], conv[BLK:, :]], axis=1
    )
    normed[...] = total
    tp_out[0] = row_sums(total * total)
    loop(1, n_tp, lambda r: tp_copy(0, r).start())
    for piece in (0, 1):
        send_x(K, piece)

    def chip_tile(t, r):
        return big[t, jnp.where(r % 2 == a, x, 4), r // 2]

    def x_tile(t, slot):
        return big[t, slot].reshape(2 * BLK, HD)

    neg = jnp.full((4, 2 * BLK), FILL, F32)
    ml[x, 0:4] = neg
    ml[x, 4:8] = jnp.zeros_like(neg)

    def key_scores(xq, own):
        queries = x_tile(Q, xq)
        top = jnp.full((1, 2 * BLK), FILL, F32)
        for r in range(4):
            s = dot_nt(chip_tile(K, r), queries) * (scale * LOG2E)
            if own:
                s = jnp.where(rel[...] >= BLK * r, s, FILL)
            work[r] = s
            top = jnp.maximum(top, jnp.max(s, axis=0, keepdims=True))
        total = jnp.zeros((1, 2 * BLK), F32)
        for r in range(4):
            e = jnp.exp2(work[r] - top)
            exps[xq, r] = e.astype(BF16)
            total = total + jnp.sum(e, axis=0, keepdims=True)
        ml[x, pl.ds(xq, 1)] = top
        ml[x, pl.ds(4 + xq, 1)] = total

    for piece in (0, 1):
        piece_wait(K, piece, 4)
    key_scores(x, True)

    def later_scores(xq):
        for piece in (0, 1):
            piece_wait(Q, piece, xq)
        key_scores(xq, False)

    loop(x + 1, NX, later_scores)

    def stat_copy(buf, send, recv, to):
        return remote(buf.at[x], buf.at[x], send.at[to], recv.at[x], ctx=4 * to + mine)

    def stat_wait(buf, send, recv, src):
        remote(buf.at[src], buf.at[src], send.at[src], recv.at[src], ctx=4 * src + mine).wait_recv()

    def others(body):
        loop(1, NX, lambda r: body(lax.rem(x + r, NX)))

    others(lambda to: stat_copy(ml, ml_s, ml_r, to).start())

    def tp_total(which):
        tp_all(which).wait_recv()
        return jnp.sum(tp_in[which], axis=0) + tp_out[which]

    inverse = columns(lax.rsqrt(tp_total(0) / float(n_tp * 2 * HD) + EPS))
    inv[...] = inverse
    normed[...] = normed[...] * jnp.concatenate([inverse, inverse], axis=1)
    swap[V] = jnp.zeros((BLK, HD), BF16)
    vals = (normed[...] * gain[...]).astype(BF16)

    @pl.when(y == 0)
    def _():
        big[V, x, 0] = vals[:, :HD]
        swap[V] = vals[:, HD:]

    @pl.when(y == 1)
    def _():
        big[V, x, 1] = vals[:, HD:]
        swap[V] = vals[:, :HD]

    swap_copy(V).start()
    send_piece(V, y)

    others(lambda src: stat_wait(ml, ml_s, ml_r, src))
    tops = jnp.max(ml[:, 0:4, :], axis=0)
    sums = jnp.sum(ml[:, 4:8, :] * jnp.exp2(ml[:, 0:4, :] - tops[None]), axis=0)
    lse = tops + jnp.log2(sums)
    fs[4:8] = lse
    fs[0:4] = jnp.exp2(ml[x, 0:4] - lse)

    def sib_stat(kind):
        return remote(ls.at[kind, 0], ls.at[kind, 1], ls_s.at[kind], ls_r.at[kind], ctx=sibling)

    ls[0, 0] = fs[pl.ds(4 + x, 1)]
    sib_stat(0).start()

    def value_grads(xq, first):
        f = columns(fs[pl.ds(xq, 1)])
        cotangents = (x_tile(DO, xq).astype(F32) * f).astype(BF16)
        for r in range(4):
            part = dot(exps[xq, r], cotangents)
            acc[0, r] = part if first else acc[0, r] + part

    def later_value_grads(xq):
        for piece in (0, 1):
            piece_wait(DO, piece, xq)
        value_grads(xq, False)

    value_grads(x, True)
    loop(x + 1, NX, later_value_grads)

    def ret_copy(t, r):
        return remote(
            ret_out.at[t, r], ret_in.at[t, mine], rt_s.at[t, r], rt_r.at[t, mine], ctx=4 * x + r
        )

    def ret_wait(t, src):
        remote(
            ret_out.at[t, src], ret_in.at[t, src], rt_s.at[t, src], rt_r.at[t, src], ctx=4 * x + src
        ).wait_recv()

    def quad(body):
        loop(1, 4, lambda i: body(lax.rem(mine + i, 4)))

    def give_back(t, r, value):
        ret_out[t, r] = value.astype(BF16)

        @pl.when(r != mine)
        def _():
            ret_copy(t, r).start()

        @pl.when(r == mine)
        def _():
            ret_in[t, mine] = ret_out[t, mine]

    def take_back(t):
        quad(lambda src: ret_wait(t, src))
        return jnp.concatenate(
            [
                ret_in[t, 0].astype(F32) + ret_in[t, 1].astype(F32),
                ret_in[t, 2].astype(F32) + ret_in[t, 3].astype(F32),
            ],
            axis=1,
        )

    for r in range(4):
        give_back(R_DV, r, acc[0, r])

    swap_wait(V)
    send_piece(V, 1 - y)
    for piece in (0, 1):
        piece_wait(V, piece, 4)
    dl[x] = jnp.zeros((8, 2 * BLK), F32)

    def key_delta(xq):
        f = fs[pl.ds(xq, 1)]
        qs[xq] = (x_tile(Q, xq).astype(F32) * (columns(f) * scale)).astype(BF16)
        cotangents = x_tile(DO, xq)
        total = jnp.zeros((1, 2 * BLK), F32)
        for r in range(4):
            dp = dot_nt(chip_tile(V, r), cotangents)
            dprob[xq, r] = dp
            total = total + jnp.sum(exps[xq, r].astype(F32) * dp, axis=0, keepdims=True)
        dl[x, pl.ds(xq, 1)] = total * f

    loop(x, NX, key_delta)
    others(lambda to: stat_copy(dl, dl_s, dl_r, to).start())

    dvalues = take_back(R_DV)
    dsum[...] = dvalues * gain[...]
    tp_out[1] = row_sums(dsum[...] * normed[...])
    loop(1, n_tp, lambda r: tp_copy(1, r).start())
    gain_out[...] = jnp.sum(dvalues * normed[...], axis=0, keepdims=True)

    def gain_copy(r):
        return remote(
            gain_out, gain_in.at[n_ctx - 1 - r], ga_s.at[0], ga_r.at[0], ctx=lax.rem(b + r, n_ctx)
        )

    loop(1, n_ctx, lambda r: gain_copy(r).start())

    others(lambda src: stat_wait(dl, dl_s, dl_r, src))
    fs[0:8] = jnp.sum(dl[...], axis=0)
    ls[1, 0] = fs[pl.ds(x, 1)]
    sib_stat(1).start()

    def key_grads(xq, first):
        delta = fs[pl.ds(xq, 1)]
        for r in range(4):
            ds = exps[xq, r].astype(F32) * (dprob[xq, r] - delta)
            part = dot(ds.astype(BF16), qs[xq])
            acc[0, r] = part if first else acc[0, r] + part

    key_grads(x, True)
    loop(x + 1, NX, lambda xq: key_grads(xq, False))
    for r in range(4):
        give_back(R_DK, r, acc[0, r])

    for kind in (0, 1):
        sib_stat(kind).wait_recv()
        for who in (0, 1):
            lcol[kind, who] = columns(ls[kind, who]).reshape(2, BLK, HD)
    for t in (Q, DO):
        for piece in (0, 1):
            piece_wait(t, piece, 4)

    def earlier_wait(src):
        for t in (K, V):
            for piece in (0, 1):
                piece_wait(t, piece, src)

    loop(0, x, earlier_wait)

    def wide(col):
        return jnp.concatenate([col] * 4, axis=1)

    def query_rows(xk, own):
        keys = x_tile(K, xk)
        vals = x_tile(V, xk)
        for r in range(4):
            who = jnp.where(r % 2 == a, 0, 1)
            s = dot_nt(chip_tile(Q, r), keys) * (scale * LOG2E)
            p = jnp.exp2(s - wide(lcol[0, who, r // 2]))
            if own:
                p = jnp.where(rel[...] <= BLK * r, p, 0.0)
            dp = dot_nt(chip_tile(DO, r), vals)
            ds = p * (dp - wide(lcol[1, who, r // 2]))
            att = dot(p.astype(BF16), vals)
            dq = dot(ds.astype(BF16), keys)
            acc[0, r] = att if own else acc[0, r] + att
            acc[1, r] = dq if own else acc[1, r] + dq

    query_rows(x, True)
    loop(0, x, lambda xk: query_rows(xk, False))
    for r in range(4):
        give_back(R_ATT, r, acc[0, r])
        give_back(R_DQ, r, acc[1, r] * scale)

    dot_col = columns(tp_total(1) / float(n_tp * 2 * HD))
    inverse2 = jnp.concatenate([inv[...], inv[...]], axis=1)
    dsummed = inverse2 * (dsum[...] - normed[...] * jnp.concatenate([dot_col, dot_col], axis=1))
    stream_o[...] = dsummed.astype(BF16)
    gate_o[...] = (
        dsummed * jnp.concatenate([conv[0:BLK, :], conv[BLK:, :]], axis=1)
    ).astype(BF16)
    stores[4].start()
    stores[1].start()
    back = dsummed * gate[...].astype(F32)
    xs[0:BLK, :] = back[:, :HD]
    xs[BLK:, :] = back[:, HD:]
    filter_ends(True)
    loop(0, b, lambda dst: state_copy(1, dst).start())

    remote(gain_in, gain_in, ga_s.at[0], ga_r.at[0], ctx=sibling).wait_recv()
    gain_o[...] = jnp.sum(gain_in[...], axis=0) + gain_out[...]
    stores[5].start()
    key_o[...] = take_back(R_DK).astype(BF16)
    stores[7].start()
    att_o[...] = take_back(R_ATT).astype(BF16)
    stores[0].start()
    query_o[...] = take_back(R_DQ).astype(BF16)
    stores[6].start()

    gather_states(1)
    filter_run(True)
    dmixed = jnp.concatenate([conv[0:BLK, :], conv[BLK:, :]], axis=1)
    keyp_o[...] = (dmixed * valp[...].astype(F32)).astype(BF16)
    valp_o[...] = (dmixed * keyp[...].astype(F32)).astype(BF16)

    stores[2].start()
    stores[3].start()

    loop(b + 1, n_ctx, lambda dst: state_copy(0, dst).wait_send())
    loop(0, b, lambda dst: state_copy(1, dst).wait_send())
    for t in (Q, DO, K, V):
        swap_copy(t).wait_send()
        for piece in (0, 1):
            drain_piece(t, piece)
    for which in (0, 1):
        tp_all(which).wait_send()
        sib_stat(which).wait_send()
    remote(gain_in, gain_in, ga_s.at[0], ga_r.at[0], ctx=sibling).wait_send()
    others(lambda to: stat_copy(ml, ml_s, ml_r, to).wait_send())
    others(lambda to: stat_copy(dl, dl_s, dl_r, to).wait_send())
    for t in (R_DV, R_DK, R_ATT, R_DQ):
        quad(lambda r: ret_copy(t, r).wait_send())
    for copy in stores:
        copy.wait()


def store(*refs):
    held, sem = refs[16:24], refs[24]
    arrive = [pltpu.make_async_copy(refs[i], held[i], sem.at[0, i]) for i in range(8)]
    leave = [pltpu.make_async_copy(held[i], refs[8 + i], sem.at[1, i]) for i in range(8)]
    for copy in arrive:
        copy.start()
    for one, other in zip(arrive, leave):
        one.wait()
        other.start()
    for copy in leave:
        copy.wait()


def on_device(n_ctx, n_tp, *arrays):
    (gate, keyp, valp, stream, decay, residue, gain, query, key, grad) = arrays
    rows, chans = stream.shape
    full = jax.ShapeDtypeStruct((rows, chans), BF16)
    dma = pltpu.SemaphoreType.DMA

    def body(*refs):
        kernel(n_ctx, n_tp, *refs)

    scratch = [
        *[pltpu.VMEM((rows, chans), BF16)] * 4,
        *[pltpu.VMEM((MODES, chans), F32)] * 2,
        pltpu.VMEM((1, chans), F32),
        *[pltpu.VMEM((rows, chans), BF16)] * 3,
        *[pltpu.VMEM((rows, chans), BF16)] * 5,
        pltpu.VMEM((1, chans), F32),
        *[pltpu.VMEM((rows, chans), BF16)] * 2,
        pltpu.VMEM((2 * BLK, HD), F32),
        pltpu.VMEM((2 * BLK, HD), F32),
        *[pltpu.VMEM((MODES, 8, HD), F32)] * 6,
        pltpu.VMEM((2, MODES, 2 * HD), BF16),
        pltpu.VMEM((2, n_ctx, MODES, 2 * HD), BF16),
        pltpu.VMEM((MODES, 2 * HD), F32),
        pltpu.VMEM((2, 1, BLK), F32),
        pltpu.VMEM((2, n_tp - 1, 1, BLK), F32),
        pltpu.VMEM((1, 2 * HD), F32),
        pltpu.VMEM((n_ctx - 1, 1, 2 * HD), F32),
        pltpu.VMEM((BLK, 2 * HD), F32),
        pltpu.VMEM((BLK, HD), F32),
        pltpu.VMEM((BLK, 2 * HD), F32),
        pltpu.VMEM((4, BLK, HD), BF16),
        pltpu.VMEM((4, 5, 2, BLK, HD), BF16),
        pltpu.VMEM((NX, 4, BLK, 2 * BLK), BF16),
        pltpu.VMEM((4, BLK, 2 * BLK), F32),
        pltpu.VMEM((NX, 4, BLK, 2 * BLK), F32),
        pltpu.VMEM((BLK, 2 * BLK), jnp.int32),
        pltpu.VMEM((NX, 8, 2 * BLK), F32),
        pltpu.VMEM((NX, 8, 2 * BLK), F32),
        pltpu.VMEM((8, 2 * BLK), F32),
        pltpu.VMEM((2, 4, BLK, HD), F32),
        pltpu.VMEM((NX, 2 * BLK, HD), BF16),
        pltpu.VMEM((2, 2, 1, 2 * BLK), F32),
        pltpu.VMEM((2, 2, 2, BLK, HD), F32),
        pltpu.VMEM((4, 4, BLK, HD), BF16),
        pltpu.VMEM((4, 4, BLK, HD), BF16),
        dma((2, n_ctx)),
        dma((2, n_ctx)),
        dma((2,)),
        dma((2,)),
        dma((1,)),
        dma((1,)),
        dma((4,)),
        dma((4,)),
        dma((4, 2, 4)),
        dma((4, 2, 5)),
        dma((NX,)),
        dma((NX,)),
        dma((NX,)),
        dma((NX,)),
        dma((2,)),
        dma((2,)),
        dma((4, 4)),
        dma((4, 4)),
        dma((10,)),
        dma((8,)),
    ]
    hbm = pl.BlockSpec(memory_space=pltpu.HBM)
    shapes = (full,) * 5 + (jax.ShapeDtypeStruct((1, chans), F32),) + (full,) * 2
    outs = pl.pallas_call(
        body,
        out_shape=shapes,
        in_specs=[hbm] * 10,
        out_specs=(hbm,) * 8,
        scratch_shapes=scratch,
        compiler_params=pltpu.CompilerParams(
            collective_id=0, has_side_effects=True, vmem_limit_bytes=VMEM
        ),
    )(gate, keyp, valp, stream, decay, residue, gain.reshape(1, chans), query, key, grad)
    outs = pl.pallas_call(
        store,
        out_shape=shapes,
        in_specs=[hbm] * 8,
        out_specs=(hbm,) * 8,
        scratch_shapes=[*[pltpu.VMEM(s.shape, s.dtype) for s in shapes], dma((2, 8))],
        compiler_params=pltpu.CompilerParams(vmem_limit_bytes=VMEM),
    )(*outs)
    return outs[:5] + (outs[5].reshape(chans),) + outs[6:]


def solution(mesh):
    n_ctx, n_tp = mesh.shape["ctx"], mesh.shape["tp"]
    both = P("ctx", "tp")

    def body(*arrays):
        return on_device(n_ctx, n_tp, *arrays)

    return jax.shard_map(
        body,
        mesh=mesh,
        in_specs=(both,) * 4 + (P(None, "tp"), P(None, "tp"), P("tp")) + (both,) * 3,
        out_specs=(both,) * 5 + (P("tp"),) + (both,) * 2,
        check_vma=False,
    )
```

```python
import jax
import jax.numpy as jnp
from jax import lax
from jax.experimental import pallas as pl
from jax.experimental.pallas import tpu as pltpu
from jax.sharding import PartitionSpec as P

HD = 128
BLK = 256
MODES = 16
CHUNK = 64
NX = 4
FILL = -1e30
VMEM = 63 * 1024 * 1024
EPS = 1e-06
LOG2E = 1.4426950408889634
NT = (((1,), (1,)), ((), ()))
HIGHEST = lax.Precision.HIGHEST
F32 = jnp.float32
BF16 = jnp.bfloat16
Q, DO, K, V = 0, 1, 2, 3
R_DV, R_DK, R_ATT, R_DQ = 0, 1, 2, 3


def remote(src, dst, send, recv, **where):
    return pltpu.make_async_remote_copy(
        src_ref=src,
        dst_ref=dst,
        send_sem=send,
        recv_sem=recv,
        device_id=where,
        device_id_type=pl.DeviceIdType.MESH,
    )


def loop(lo, hi, body):
    def step(i, carry):
        body(i)
        return carry

    lax.fori_loop(lo, hi, step, 0)


def halves(row):
    return jnp.concatenate(
        [jnp.broadcast_to(row[:, :HD], (4, HD)), jnp.broadcast_to(row[:, HD:], (4, HD))], axis=0
    )


def columns(row):
    return jnp.transpose(jnp.broadcast_to(row, (HD, row.shape[1])))


def row_sums(x):
    ones = jnp.ones((8, x.shape[1]), F32)
    return lax.dot_general(ones, x, NT, precision=HIGHEST, preferred_element_type=F32)[0:1]


def dot_nt(a, b):
    return lax.dot_general(a, b, NT, preferred_element_type=F32)


def dot(a, b):
    return jnp.dot(a, b, preferred_element_type=F32)


def kernel(
    n_ctx,
    n_tp,
    gate_h,
    keyp_h,
    valp_h,
    stream_h,
    decay_h,
    residue_h,
    gain_h,
    query_h,
    key_h,
    grad_h,
    att_h,
    gateg_h,
    keypg_h,
    valpg_h,
    streamg_h,
    gaing_h,
    queryg_h,
    keyg_h,
    gate,
    keyp,
    valp,
    stream,
    decay,
    residue,
    gain,
    query,
    key,
    grad,
    att_o,
    gate_o,
    keyp_o,
    valp_o,
    stream_o,
    gain_o,
    query_o,
    key_o,
    xs,
    conv,
    fac,
    res,
    d64,
    up,
    down,
    ends,
    state_out,
    state_in,
    ein,
    tp_out,
    tp_in,
    gain_out,
    gain_in,
    normed,
    inv,
    dsum,
    swap,
    big,
    exps,
    probs,
    work,
    dprob,
    rel,
    ml,
    dl,
    fs,
    acc,
    qs,
    ls,
    lcol,
    ret_out,
    ret_in,
    st_s,
    st_r,
    tp_s,
    tp_r,
    ga_s,
    ga_r,
    sw_s,
    sw_r,
    bg_s,
    bg_r,
    ml_s,
    ml_r,
    dl_s,
    dl_r,
    ls_s,
    ls_r,
    rt_s,
    rt_r,
    in_s,
    out_s,
):
    b = lax.axis_index("ctx")
    tp = lax.axis_index("tp")
    x = b // 4
    y = (b // 2) % 2
    a = b % 2
    mine = b % 4
    sibling = b + 1 - 2 * a
    across = b + 2 - 4 * y
    scale = HD**-0.5

    loads = [
        pltpu.make_async_copy(src, dst, in_s.at[i])
        for i, (src, dst) in enumerate(
            (
                (decay_h, decay),
                (residue_h, residue),
                (keyp_h, keyp),
                (valp_h, valp),
                (query_h, query),
                (grad_h, grad),
                (key_h, key),
                (gate_h, gate),
                (stream_h, stream),
                (gain_h, gain),
            )
        )
    ]
    for load in loads:
        load.start()

    results = (
        (att_o, att_h),
        (gate_o, gateg_h),
        (keyp_o, keypg_h),
        (valp_o, valpg_h),
        (stream_o, streamg_h),
        (gain_o, gaing_h),
        (query_o, queryg_h),
        (key_o, keyg_h),
    )
    stores = [pltpu.make_async_copy(v, h, out_s.at[i]) for i, (v, h) in enumerate(results)]

    barrier = pltpu.get_barrier_semaphore()

    def greet_ctx(r):
        pl.semaphore_signal(
            barrier, 1, device_id={"ctx": lax.rem(b + r, n_ctx)}, device_id_type=pl.DeviceIdType.MESH
        )

    def greet_tp(r):
        pl.semaphore_signal(
            barrier, 1, device_id={"tp": lax.rem(tp + r, n_tp)}, device_id_type=pl.DeviceIdType.MESH
        )

    half = n_tp // 2
    for r in sorted(range(1, n_tp), key=lambda r: -min(r % half, half - r % half)):
        greet_tp(r)
    for r in range(1, n_ctx):
        greet_ctx(r)

    for load in loads[:2]:
        load.wait()
    chunk_id = lax.broadcasted_iota(jnp.int32, (8, HD), 0) % 4
    chunk_f = chunk_id.astype(F32)
    for m in range(MODES):
        rate = halves(decay[m : m + 1, :])
        fac[m] = jnp.exp(-rate)
        res[m] = halves(residue[m : m + 1, :])
        d64[m] = jnp.exp(-CHUNK * rate)
        up[m] = jnp.exp(-CHUNK * rate * chunk_f)
        down[m] = jnp.exp(-CHUNK * rate * (3.0 - chunk_f))
    d256 = jnp.exp(-float(BLK) * decay[...])

    def filter_ends(backward):
        factors = [fac[m] for m in range(MODES)]

        def step(t, states):
            at = CHUNK - 1 - t if backward else t
            column = xs[pl.ds(at, 8, stride=CHUNK), :]
            return tuple(f * s + column for f, s in zip(factors, states))

        zero = jnp.zeros((8, HD), F32)
        states = lax.fori_loop(0, CHUNK, step, (zero,) * MODES, unroll=4)
        weight = up if backward else down
        for m in range(MODES):
            ends[m] = states[m]
            part = states[m] * weight[m]
            ein[m : m + 1, 0:HD] = jnp.sum(part[0:4], axis=0, keepdims=True)
            ein[m : m + 1, HD : 2 * HD] = jnp.sum(part[4:8], axis=0, keepdims=True)
        state_out[int(backward)] = ein[...].astype(BF16)

    def filter_run(backward):
        factors = [fac[m] for m in range(MODES)]
        weights = [res[m] for m in range(MODES)]
        reach = down if backward else up
        entries = []
        for m in range(MODES):
            end = ends[m]
            total = reach[m] * halves(ein[m : m + 1, :])
            power = jnp.ones((8, HD), F32)
            for back in (1, 2, 3):
                moved = pltpu.roll(end, 8 - back if backward else back, 0)
                ok = chunk_id <= 3 - back if backward else chunk_id >= back
                total = total + power * jnp.where(ok, moved, 0.0)
                power = power * d64[m]
            entries.append(total)

        def step(t, states):
            at = CHUNK - 1 - t if backward else t
            column = xs[pl.ds(at, 8, stride=CHUNK), :]
            states = tuple(f * s + column for f, s in zip(factors, states))
            terms = [w * s for w, s in zip(weights, states)]
            while len(terms) > 1:
                terms = [u + v for u, v in zip(terms[::2], terms[1::2])]
            conv[pl.ds(at, 8, stride=CHUNK), :] = terms[0]
            return states

        lax.fori_loop(0, CHUNK, step, tuple(entries), unroll=2)

    def state_copy(way, dst):
        return remote(
            state_out.at[way], state_in.at[way, b], st_s.at[way, dst], st_r.at[way, b], ctx=dst
        )

    def state_wait(way, src):
        remote(
            state_out.at[way], state_in.at[way, src], st_s.at[way, src], st_r.at[way, src], ctx=src
        ).wait_recv()

    for load in loads[2:4]:
        load.wait()
    mixed = keyp[...].astype(F32) * valp[...].astype(F32)
    xs[0:BLK, :] = mixed[:, :HD]
    xs[BLK:, :] = mixed[:, HD:]
    filter_ends(False)

    def place(t, array):
        big[t, x, y] = array[:, pl.ds(pl.multiple_of(y * HD, HD), HD)]
        swap[t] = array[:, pl.ds(pl.multiple_of((1 - y) * HD, HD), HD)]

    def swap_copy(t):
        return remote(swap.at[t], big.at[t, x, y], sw_s.at[t], sw_r.at[t], ctx=across)

    def swap_wait(t):
        remote(swap.at[t], big.at[t, x, 1 - y], sw_s.at[t], sw_r.at[t], ctx=across).wait_recv()

    def x_copy(t, piece, to):
        return remote(
            big.at[t, x, piece],
            big.at[t, x, piece],
            bg_s.at[t, piece, to],
            bg_r.at[t, piece, x],
            ctx=4 * to + mine,
        )

    def sib_copy(t, piece):
        return remote(
            big.at[t, x, piece],
            big.at[t, 4, piece],
            bg_s.at[t, piece, x],
            bg_r.at[t, piece, 4],
            ctx=sibling,
        )

    def piece_wait(t, piece, slot):
        remote(
            big.at[t, x, piece],
            big.at[t, slot, piece],
            bg_s.at[t, piece, slot % 4],
            bg_r.at[t, piece, slot],
            ctx=sibling,
        ).wait_recv()

    def targets(t, body):
        if t in (Q, DO):
            loop(0, x, lambda i: body(x - 1 - i))
        else:
            loop(x + 1, NX, body)

    def send_x(t, piece):
        targets(t, lambda to: x_copy(t, piece, to).start())

    def send_piece(t, piece):
        sib_copy(t, piece).start()
        send_x(t, piece)

    def drain_piece(t, piece):
        sib_copy(t, piece).wait_send()
        targets(t, lambda to: x_copy(t, piece, to).wait_send())

    for load in loads[4:7]:
        load.wait()
    place(Q, query)
    place(DO, grad)
    place(K, key)
    rel[...] = (
        lax.broadcasted_iota(jnp.int32, (BLK, 2 * BLK), 1)
        + BLK * (lax.broadcasted_iota(jnp.int32, (BLK, 2 * BLK), 1) // BLK)
        + BLK * a
        - lax.broadcasted_iota(jnp.int32, (BLK, 2 * BLK), 0)
    )

    pl.semaphore_wait(barrier, n_ctx + n_tp - 2)

    swap_copy(Q).start()
    swap_copy(K).start()
    send_x(Q, y)
    sib_copy(K, y).start()
    loop(b + 1, n_ctx, lambda dst: state_copy(0, dst).start())
    swap_copy(DO).start()
    swap_wait(Q)
    send_x(Q, 1 - y)
    swap_wait(K)
    sib_copy(K, 1 - y).start()
    send_piece(DO, y)
    swap_wait(DO)
    send_piece(DO, 1 - y)
    for piece in (0, 1):
        sib_copy(Q, piece).start()

    def gather_states(way):
        def hop(i, total):
            src = n_ctx - 1 - i if way else i
            state_wait(way, src)
            return d256 * total + state_in[way, src].astype(F32)

        count = n_ctx - 1 - b if way else b
        ein[...] = lax.fori_loop(0, count, hop, jnp.zeros((MODES, 2 * HD), F32))

    def tp_copy(which, r):
        return remote(
            tp_out.at[which],
            tp_in.at[which, n_tp - 1 - r],
            tp_s.at[which],
            tp_r.at[which],
            tp=lax.rem(tp + r, n_tp),
        )

    def tp_all(which):
        return remote(
            tp_in.at[which], tp_in.at[which], tp_s.at[which], tp_r.at[which], tp=lax.rem(tp + 1, n_tp)
        )

    for load in loads[7:]:
        load.wait()
    gather_states(0)
    filter_run(False)
    total = stream[...].astype(F32) + gate[...].astype(F32) * jnp.concatenate(
        [conv[0:BLK, :], conv[BLK:, :]], axis=1
    )
    normed[...] = total
    tp_out[0] = row_sums(total * total)
    loop(1, n_tp, lambda r: tp_copy(0, r).start())
    for piece in (0, 1):
        send_x(K, piece)

    def chip_tile(t, r):
        return big[t, jnp.where(r % 2 == a, x, 4), r // 2]

    def x_tile(t, slot):
        return big[t, slot].reshape(2 * BLK, HD)

    neg = jnp.full((4, 2 * BLK), FILL, F32)
    ml[x, 0:4] = neg
    ml[x, 4:8] = jnp.zeros_like(neg)

    def key_scores(xq, own):
        queries = x_tile(Q, xq)
        top = jnp.full((1, 2 * BLK), FILL, F32)
        for r in range(4):
            s = dot_nt(chip_tile(K, r), queries) * (scale * LOG2E)
            if own:
                s = jnp.where(rel[...] >= BLK * r, s, FILL)
            work[r] = s
            top = jnp.maximum(top, jnp.max(s, axis=0, keepdims=True))
        total = jnp.zeros((1, 2 * BLK), F32)
        for r in range(4):
            e = jnp.exp2(work[r] - top)
            exps[xq, r] = e.astype(BF16)
            total = total + jnp.sum(e, axis=0, keepdims=True)
        ml[x, pl.ds(xq, 1)] = top
        ml[x, pl.ds(4 + xq, 1)] = total

    for piece in (0, 1):
        piece_wait(K, piece, 4)
    key_scores(x, True)

    def later_scores(xq):
        for piece in (0, 1):
            piece_wait(Q, piece, xq)
        key_scores(xq, False)

    loop(x + 1, NX, later_scores)

    def stat_copy(buf, send, recv, to):
        return remote(buf.at[x], buf.at[x], send.at[to], recv.at[x], ctx=4 * to + mine)

    def stat_wait(buf, send, recv, src):
        remote(buf.at[src], buf.at[src], send.at[src], recv.at[src], ctx=4 * src + mine).wait_recv()

    def others(body):
        loop(1, NX, lambda r: body(lax.rem(x + r, NX)))

    others(lambda to: stat_copy(ml, ml_s, ml_r, to).start())

    def tp_total(which):
        tp_all(which).wait_recv()
        return jnp.sum(tp_in[which], axis=0) + tp_out[which]

    inverse = columns(lax.rsqrt(tp_total(0) / float(n_tp * 2 * HD) + EPS))
    inv[...] = inverse
    normed[...] = normed[...] * jnp.concatenate([inverse, inverse], axis=1)
    swap[V] = jnp.zeros((BLK, HD), BF16)
    vals = (normed[...] * gain[...]).astype(BF16)

    @pl.when(y == 0)
    def _():
        big[V, x, 0] = vals[:, :HD]
        swap[V] = vals[:, HD:]

    @pl.when(y == 1)
    def _():
        big[V, x, 1] = vals[:, HD:]
        swap[V] = vals[:, :HD]

    swap_copy(V).start()
    send_piece(V, y)

    others(lambda src: stat_wait(ml, ml_s, ml_r, src))
    tops = jnp.max(ml[:, 0:4, :], axis=0)
    sums = jnp.sum(ml[:, 4:8, :] * jnp.exp2(ml[:, 0:4, :] - tops[None]), axis=0)
    lse = tops + jnp.log2(sums)
    fs[4:8] = lse
    fs[0:4] = jnp.exp2(ml[x, 0:4] - lse)

    def sib_stat(kind):
        return remote(ls.at[kind, 0], ls.at[kind, 1], ls_s.at[kind], ls_r.at[kind], ctx=sibling)

    ls[0, 0] = fs[pl.ds(4 + x, 1)]
    sib_stat(0).start()

    def value_grads(xq, first):
        f = columns(fs[pl.ds(xq, 1)])
        cotangents = (x_tile(DO, xq).astype(F32) * f).astype(BF16)
        for r in range(4):
            part = dot(exps[xq, r], cotangents)
            acc[0, r] = part if first else acc[0, r] + part

    def later_value_grads(xq):
        for piece in (0, 1):
            piece_wait(DO, piece, xq)
        value_grads(xq, False)

    value_grads(x, True)
    loop(x + 1, NX, later_value_grads)

    def ret_copy(t, r):
        return remote(
            ret_out.at[t, r], ret_in.at[t, mine], rt_s.at[t, r], rt_r.at[t, mine], ctx=4 * x + r
        )

    def ret_wait(t, src):
        remote(
            ret_out.at[t, src], ret_in.at[t, src], rt_s.at[t, src], rt_r.at[t, src], ctx=4 * x + src
        ).wait_recv()

    def quad(body):
        loop(1, 4, lambda i: body(lax.rem(mine + i, 4)))

    def give_back(t, r, value):
        ret_out[t, r] = value.astype(BF16)

        @pl.when(r != mine)
        def _():
            ret_copy(t, r).start()

        @pl.when(r == mine)
        def _():
            ret_in[t, mine] = ret_out[t, mine]

    def take_back(t):
        quad(lambda src: ret_wait(t, src))
        return jnp.concatenate(
            [
                ret_in[t, 0].astype(F32) + ret_in[t, 1].astype(F32),
                ret_in[t, 2].astype(F32) + ret_in[t, 3].astype(F32),
            ],
            axis=1,
        )

    for r in range(4):
        give_back(R_DV, r, acc[0, r])

    swap_wait(V)
    send_piece(V, 1 - y)
    for piece in (0, 1):
        piece_wait(V, piece, 4)
    dl[x] = jnp.zeros((8, 2 * BLK), F32)

    def key_delta(xq):
        f = fs[pl.ds(xq, 1)]
        qs[xq] = (x_tile(Q, xq).astype(F32) * (columns(f) * scale)).astype(BF16)
        cotangents = x_tile(DO, xq)
        total = jnp.zeros((1, 2 * BLK), F32)
        for r in range(4):
            dp = dot_nt(chip_tile(V, r), cotangents)
            dprob[xq, r] = dp
            total = total + jnp.sum(exps[xq, r].astype(F32) * dp, axis=0, keepdims=True)
        dl[x, pl.ds(xq, 1)] = total * f

    loop(x, NX, key_delta)
    others(lambda to: stat_copy(dl, dl_s, dl_r, to).start())

    def wide(col):
        return jnp.concatenate([col] * 4, axis=1)

    def side(r):
        return jnp.where(r % 2 == a, 0, 1)

    sib_stat(0).wait_recv()
    for who in (0, 1):
        lcol[0, who] = columns(ls[0, who]).reshape(2, BLK, HD)
    for piece in (0, 1):
        piece_wait(Q, piece, 4)

    def query_probs(xk, own):
        keys = x_tile(K, xk)
        for r in range(4):
            s = dot_nt(chip_tile(Q, r), keys) * (scale * LOG2E)
            p = jnp.exp2(s - wide(lcol[0, side(r), r // 2]))
            if own:
                p = jnp.where(rel[...] <= BLK * r, p, 0.0)
            probs[xk, r] = p.astype(BF16)

    def earlier_probs(xk):
        for piece in (0, 1):
            piece_wait(K, piece, xk)
        query_probs(xk, False)

    query_probs(x, True)
    loop(0, x, earlier_probs)

    loop(b + 1, n_ctx, lambda dst: state_copy(0, dst).wait_send())
    for t in (Q, DO, K, V):
        swap_copy(t).wait_send()
    for t in (Q, DO, K):
        for piece in (0, 1):
            drain_piece(t, piece)
    tp_all(0).wait_send()
    sib_stat(0).wait_send()
    others(lambda to: stat_copy(ml, ml_s, ml_r, to).wait_send())

    dvalues = take_back(R_DV)
    dsum[...] = dvalues * gain[...]
    tp_out[1] = row_sums(dsum[...] * normed[...])
    loop(1, n_tp, lambda r: tp_copy(1, r).start())
    gain_out[...] = jnp.sum(dvalues * normed[...], axis=0, keepdims=True)

    def gain_copy(r):
        return remote(
            gain_out, gain_in.at[n_ctx - 1 - r], ga_s.at[0], ga_r.at[0], ctx=lax.rem(b + r, n_ctx)
        )

    loop(1, n_ctx, lambda r: gain_copy(r).start())

    others(lambda src: stat_wait(dl, dl_s, dl_r, src))
    fs[0:8] = jnp.sum(dl[...], axis=0)
    ls[1, 0] = fs[pl.ds(x, 1)]
    sib_stat(1).start()

    def key_grads(xq, first):
        delta = fs[pl.ds(xq, 1)]
        for r in range(4):
            ds = exps[xq, r].astype(F32) * (dprob[xq, r] - delta)
            part = dot(ds.astype(BF16), qs[xq])
            acc[0, r] = part if first else acc[0, r] + part

    sib_stat(1).wait_recv()
    for who in (0, 1):
        lcol[1, who] = columns(ls[1, who]).reshape(2, BLK, HD)
    for piece in (0, 1):
        piece_wait(DO, piece, 4)

    def query_rows(xk, own):
        keys = x_tile(K, xk)
        vals = x_tile(V, xk)
        for r in range(4):
            p = probs[xk, r]
            dp = dot_nt(chip_tile(DO, r), vals)
            ds = p.astype(F32) * (dp - wide(lcol[1, side(r), r // 2]))
            att = dot(p, vals)
            dq = dot(ds.astype(BF16), keys)
            acc[0, r] = att if own else acc[0, r] + att
            acc[1, r] = dq if own else acc[1, r] + dq

    def earlier_rows(xk):
        for piece in (0, 1):
            piece_wait(V, piece, xk)
        query_rows(xk, False)

    def all_key_grads():
        key_grads(x, True)
        loop(x + 1, NX, lambda xq: key_grads(xq, False))
        for r in range(4):
            give_back(R_DK, r, acc[0, r])

    def all_query_rows():
        query_rows(x, True)
        loop(0, x, earlier_rows)
        for r in range(4):
            give_back(R_ATT, r, acc[0, r])
            give_back(R_DQ, r, acc[1, r] * scale)

    pl.when(x < NX // 2)(all_key_grads)
    pl.when(x >= NX // 2)(all_query_rows)

    dot_col = columns(tp_total(1) / float(n_tp * 2 * HD))
    inverse2 = jnp.concatenate([inv[...], inv[...]], axis=1)
    dsummed = inverse2 * (dsum[...] - normed[...] * jnp.concatenate([dot_col, dot_col], axis=1))
    back = dsummed * gate[...].astype(F32)
    xs[0:BLK, :] = back[:, :HD]
    xs[BLK:, :] = back[:, HD:]
    filter_ends(True)
    loop(0, b, lambda dst: state_copy(1, dst).start())
    stream_o[...] = dsummed.astype(BF16)
    gate_o[...] = (
        dsummed * jnp.concatenate([conv[0:BLK, :], conv[BLK:, :]], axis=1)
    ).astype(BF16)
    stores[4].start()
    stores[1].start()

    pl.when(x < NX // 2)(all_query_rows)
    pl.when(x >= NX // 2)(all_key_grads)

    for piece in (0, 1):
        drain_piece(V, piece)
    tp_all(1).wait_send()
    sib_stat(1).wait_send()
    remote(gain_in, gain_in, ga_s.at[0], ga_r.at[0], ctx=sibling).wait_send()
    others(lambda to: stat_copy(dl, dl_s, dl_r, to).wait_send())
    quad(lambda r: ret_copy(R_DV, r).wait_send())

    gather_states(1)
    filter_run(True)
    dmixed = jnp.concatenate([conv[0:BLK, :], conv[BLK:, :]], axis=1)
    keyp_o[...] = (dmixed * valp[...].astype(F32)).astype(BF16)
    valp_o[...] = (dmixed * keyp[...].astype(F32)).astype(BF16)

    stores[2].start()
    stores[3].start()

    remote(gain_in, gain_in, ga_s.at[0], ga_r.at[0], ctx=sibling).wait_recv()
    gain_o[...] = jnp.sum(gain_in[...], axis=0) + gain_out[...]
    stores[5].start()
    key_o[...] = take_back(R_DK).astype(BF16)
    stores[7].start()
    att_o[...] = take_back(R_ATT).astype(BF16)
    stores[0].start()
    query_o[...] = take_back(R_DQ).astype(BF16)
    stores[6].start()

    loop(0, b, lambda dst: state_copy(1, dst).wait_send())
    for t in (R_DK, R_ATT, R_DQ):
        quad(lambda r: ret_copy(t, r).wait_send())
    for copy in stores:
        copy.wait()


def store(*refs):
    held, sem = refs[16:24], refs[24]
    arrive = [pltpu.make_async_copy(refs[i], held[i], sem.at[0, i]) for i in range(8)]
    leave = [pltpu.make_async_copy(held[i], refs[8 + i], sem.at[1, i]) for i in range(8)]
    for copy in arrive:
        copy.start()
    for one, other in zip(arrive, leave):
        one.wait()
        other.start()
    for copy in leave:
        copy.wait()


def on_device(n_ctx, n_tp, *arrays):
    (gate, keyp, valp, stream, decay, residue, gain, query, key, grad) = arrays
    rows, chans = stream.shape
    full = jax.ShapeDtypeStruct((rows, chans), BF16)
    dma = pltpu.SemaphoreType.DMA

    def body(*refs):
        kernel(n_ctx, n_tp, *refs)

    scratch = [
        *[pltpu.VMEM((rows, chans), BF16)] * 4,
        *[pltpu.VMEM((MODES, chans), F32)] * 2,
        pltpu.VMEM((1, chans), F32),
        *[pltpu.VMEM((rows, chans), BF16)] * 3,
        *[pltpu.VMEM((rows, chans), BF16)] * 5,
        pltpu.VMEM((1, chans), F32),
        *[pltpu.VMEM((rows, chans), BF16)] * 2,
        pltpu.VMEM((2 * BLK, HD), F32),
        pltpu.VMEM((2 * BLK, HD), F32),
        *[pltpu.VMEM((MODES, 8, HD), F32)] * 6,
        pltpu.VMEM((2, MODES, 2 * HD), BF16),
        pltpu.VMEM((2, n_ctx, MODES, 2 * HD), BF16),
        pltpu.VMEM((MODES, 2 * HD), F32),
        pltpu.VMEM((2, 1, BLK), F32),
        pltpu.VMEM((2, n_tp - 1, 1, BLK), F32),
        pltpu.VMEM((1, 2 * HD), F32),
        pltpu.VMEM((n_ctx - 1, 1, 2 * HD), F32),
        pltpu.VMEM((BLK, 2 * HD), F32),
        pltpu.VMEM((BLK, HD), F32),
        pltpu.VMEM((BLK, 2 * HD), F32),
        pltpu.VMEM((4, BLK, HD), BF16),
        pltpu.VMEM((4, 5, 2, BLK, HD), BF16),
        pltpu.VMEM((NX, 4, BLK, 2 * BLK), BF16),
        pltpu.VMEM((NX, 4, BLK, 2 * BLK), BF16),
        pltpu.VMEM((4, BLK, 2 * BLK), F32),
        pltpu.VMEM((NX, 4, BLK, 2 * BLK), F32),
        pltpu.VMEM((BLK, 2 * BLK), jnp.int32),
        pltpu.VMEM((NX, 8, 2 * BLK), F32),
        pltpu.VMEM((NX, 8, 2 * BLK), F32),
        pltpu.VMEM((8, 2 * BLK), F32),
        pltpu.VMEM((2, 4, BLK, HD), F32),
        pltpu.VMEM((NX, 2 * BLK, HD), BF16),
        pltpu.VMEM((2, 2, 1, 2 * BLK), F32),
        pltpu.VMEM((2, 2, 2, BLK, HD), F32),
        pltpu.VMEM((4, 4, BLK, HD), BF16),
        pltpu.VMEM((4, 4, BLK, HD), BF16),
        dma((2, n_ctx)),
        dma((2, n_ctx)),
        dma((2,)),
        dma((2,)),
        dma((1,)),
        dma((1,)),
        dma((4,)),
        dma((4,)),
        dma((4, 2, 4)),
        dma((4, 2, 5)),
        dma((NX,)),
        dma((NX,)),
        dma((NX,)),
        dma((NX,)),
        dma((2,)),
        dma((2,)),
        dma((4, 4)),
        dma((4, 4)),
        dma((10,)),
        dma((8,)),
    ]
    hbm = pl.BlockSpec(memory_space=pltpu.HBM)
    shapes = (full,) * 5 + (jax.ShapeDtypeStruct((1, chans), F32),) + (full,) * 2
    outs = pl.pallas_call(
        body,
        out_shape=shapes,
        in_specs=[hbm] * 10,
        out_specs=(hbm,) * 8,
        scratch_shapes=scratch,
        compiler_params=pltpu.CompilerParams(
            collective_id=0, has_side_effects=True, vmem_limit_bytes=VMEM
        ),
    )(gate, keyp, valp, stream, decay, residue, gain.reshape(1, chans), query, key, grad)
    outs = pl.pallas_call(
        store,
        out_shape=shapes,
        in_specs=[hbm] * 8,
        out_specs=(hbm,) * 8,
        scratch_shapes=[*[pltpu.VMEM(s.shape, s.dtype) for s in shapes], dma((2, 8))],
        compiler_params=pltpu.CompilerParams(vmem_limit_bytes=VMEM),
    )(*outs)
    return outs[:5] + (outs[5].reshape(chans),) + outs[6:]


def solution(mesh):
    n_ctx, n_tp = mesh.shape["ctx"], mesh.shape["tp"]
    both = P("ctx", "tp")

    def body(*arrays):
        return on_device(n_ctx, n_tp, *arrays)

    return jax.shard_map(
        body,
        mesh=mesh,
        in_specs=(both,) * 4 + (P(None, "tp"), P(None, "tp"), P("tp")) + (both,) * 3,
        out_specs=(both,) * 5 + (P("tp"),) + (both,) * 2,
        check_vma=False,
    )
```

```python
import jax
import jax.numpy as jnp
from jax import lax
from jax.experimental import pallas as pl
from jax.experimental.pallas import tpu as pltpu
from jax.sharding import PartitionSpec as P

HD = 128
BLK = 256
MODES = 16
CHUNK = 64
NX = 4
FILL = -1e30
VMEM = 63 * 1024 * 1024
EPS = 1e-06
LOG2E = 1.4426950408889634
NT = (((1,), (1,)), ((), ()))
HIGHEST = lax.Precision.HIGHEST
F32 = jnp.float32
BF16 = jnp.bfloat16
Q, DO, K, V = 0, 1, 2, 3
R_DV, R_DK, R_ATT, R_DQ = 0, 1, 2, 3


def remote(src, dst, send, recv, **where):
    return pltpu.make_async_remote_copy(
        src_ref=src,
        dst_ref=dst,
        send_sem=send,
        recv_sem=recv,
        device_id=where,
        device_id_type=pl.DeviceIdType.MESH,
    )


def loop(lo, hi, body):
    def step(i, carry):
        body(i)
        return carry

    lax.fori_loop(lo, hi, step, 0)


def halves(row):
    return jnp.concatenate(
        [jnp.broadcast_to(row[:, :HD], (4, HD)), jnp.broadcast_to(row[:, HD:], (4, HD))], axis=0
    )


def columns(row):
    return jnp.transpose(jnp.broadcast_to(row, (HD, row.shape[1])))


def row_sums(x):
    ones = jnp.ones((8, x.shape[1]), F32)
    return lax.dot_general(ones, x, NT, precision=HIGHEST, preferred_element_type=F32)[0:1]


def dot_nt(a, b):
    return lax.dot_general(a, b, NT, preferred_element_type=F32)


def dot(a, b):
    return jnp.dot(a, b, preferred_element_type=F32)


def kernel(
    n_ctx,
    n_tp,
    gate_h,
    keyp_h,
    valp_h,
    stream_h,
    decay_h,
    residue_h,
    gain_h,
    query_h,
    key_h,
    grad_h,
    att_h,
    gateg_h,
    keypg_h,
    valpg_h,
    streamg_h,
    gaing_h,
    queryg_h,
    keyg_h,
    gate,
    keyp,
    valp,
    stream,
    decay,
    residue,
    gain,
    query,
    key,
    grad,
    att_o,
    gate_o,
    keyp_o,
    valp_o,
    stream_o,
    gain_o,
    query_o,
    key_o,
    xs,
    conv,
    fac,
    res,
    d64,
    up,
    down,
    ends,
    state_out,
    state_in,
    ein,
    tp_out,
    tp_in,
    gain_out,
    gain_in,
    normed,
    inv,
    dsum,
    swap,
    big,
    exps,
    probs,
    work,
    dprob,
    rel,
    ml,
    dl,
    fs,
    dos,
    acc,
    qs,
    ls,
    lcol,
    ret_out,
    ret_in,
    st_s,
    st_r,
    tp_s,
    tp_r,
    ga_s,
    ga_r,
    sw_s,
    sw_r,
    bg_s,
    bg_r,
    ml_s,
    ml_r,
    dl_s,
    dl_r,
    ls_s,
    ls_r,
    rt_s,
    rt_r,
    in_s,
    out_s,
):
    b = lax.axis_index("ctx")
    tp = lax.axis_index("tp")
    x = b // 4
    y = (b // 2) % 2
    a = b % 2
    mine = b % 4
    sibling = b + 1 - 2 * a
    across = b + 2 - 4 * y
    scale = HD**-0.5

    loads = [
        pltpu.make_async_copy(src, dst, in_s.at[i])
        for i, (src, dst) in enumerate(
            (
                (decay_h, decay),
                (residue_h, residue),
                (keyp_h, keyp),
                (valp_h, valp),
                (query_h, query),
                (grad_h, grad),
                (key_h, key),
                (gate_h, gate),
                (stream_h, stream),
                (gain_h, gain),
            )
        )
    ]
    for load in loads:
        load.start()

    results = (
        (att_o, att_h),
        (gate_o, gateg_h),
        (keyp_o, keypg_h),
        (valp_o, valpg_h),
        (stream_o, streamg_h),
        (gain_o, gaing_h),
        (query_o, queryg_h),
        (key_o, keyg_h),
    )
    stores = [pltpu.make_async_copy(v, h, out_s.at[i]) for i, (v, h) in enumerate(results)]

    barrier = pltpu.get_barrier_semaphore()

    def greet_ctx(r):
        pl.semaphore_signal(
            barrier, 1, device_id={"ctx": lax.rem(b + r, n_ctx)}, device_id_type=pl.DeviceIdType.MESH
        )

    def greet_tp(r):
        pl.semaphore_signal(
            barrier, 1, device_id={"tp": lax.rem(tp + r, n_tp)}, device_id_type=pl.DeviceIdType.MESH
        )

    half = n_tp // 2
    for r in sorted(range(1, n_tp), key=lambda r: -min(r % half, half - r % half)):
        greet_tp(r)
    for r in range(1, n_ctx):
        greet_ctx(r)

    for load in loads[:2]:
        load.wait()
    chunk_id = lax.broadcasted_iota(jnp.int32, (8, HD), 0) % 4
    chunk_f = chunk_id.astype(F32)
    for m in range(MODES):
        rate = halves(decay[m : m + 1, :])
        fac[m] = jnp.exp(-rate)
        res[m] = halves(residue[m : m + 1, :])
        d64[m] = jnp.exp(-CHUNK * rate)
        up[m] = jnp.exp(-CHUNK * rate * chunk_f)
        down[m] = jnp.exp(-CHUNK * rate * (3.0 - chunk_f))
    d256 = jnp.exp(-float(BLK) * decay[...])

    def filter_ends(backward):
        factors = [fac[m] for m in range(MODES)]

        def step(t, states):
            at = CHUNK - 1 - t if backward else t
            column = xs[pl.ds(at, 8, stride=CHUNK), :]
            return tuple(f * s + column for f, s in zip(factors, states))

        zero = jnp.zeros((8, HD), F32)
        states = lax.fori_loop(0, CHUNK, step, (zero,) * MODES, unroll=4)
        weight = up if backward else down
        for m in range(MODES):
            ends[m] = states[m]
            part = states[m] * weight[m]
            ein[m : m + 1, 0:HD] = jnp.sum(part[0:4], axis=0, keepdims=True)
            ein[m : m + 1, HD : 2 * HD] = jnp.sum(part[4:8], axis=0, keepdims=True)
        state_out[int(backward)] = ein[...].astype(BF16)

    def filter_run(backward):
        factors = [fac[m] for m in range(MODES)]
        weights = [res[m] for m in range(MODES)]
        reach = down if backward else up
        entries = []
        for m in range(MODES):
            end = ends[m]
            total = reach[m] * halves(ein[m : m + 1, :])
            power = jnp.ones((8, HD), F32)
            for back in (1, 2, 3):
                moved = pltpu.roll(end, 8 - back if backward else back, 0)
                ok = chunk_id <= 3 - back if backward else chunk_id >= back
                total = total + power * jnp.where(ok, moved, 0.0)
                power = power * d64[m]
            entries.append(total)

        def step(t, states):
            at = CHUNK - 1 - t if backward else t
            column = xs[pl.ds(at, 8, stride=CHUNK), :]
            states = tuple(f * s + column for f, s in zip(factors, states))
            terms = [w * s for w, s in zip(weights, states)]
            while len(terms) > 1:
                terms = [u + v for u, v in zip(terms[::2], terms[1::2])]
            conv[pl.ds(at, 8, stride=CHUNK), :] = terms[0]
            return states

        lax.fori_loop(0, CHUNK, step, tuple(entries), unroll=2)

    def state_copy(way, dst):
        return remote(
            state_out.at[way], state_in.at[way, b], st_s.at[way, dst], st_r.at[way, b], ctx=dst
        )

    def state_wait(way, src):
        remote(
            state_out.at[way], state_in.at[way, src], st_s.at[way, src], st_r.at[way, src], ctx=src
        ).wait_recv()

    for load in loads[2:4]:
        load.wait()
    mixed = keyp[...].astype(F32) * valp[...].astype(F32)
    xs[0:BLK, :] = mixed[:, :HD]
    xs[BLK:, :] = mixed[:, HD:]
    filter_ends(False)

    def place(t, array):
        big[t, x, y] = array[:, pl.ds(pl.multiple_of(y * HD, HD), HD)]
        swap[t] = array[:, pl.ds(pl.multiple_of((1 - y) * HD, HD), HD)]

    def swap_copy(t):
        return remote(swap.at[t], big.at[t, x, y], sw_s.at[t], sw_r.at[t], ctx=across)

    def swap_wait(t):
        remote(swap.at[t], big.at[t, x, 1 - y], sw_s.at[t], sw_r.at[t], ctx=across).wait_recv()

    def x_copy(t, piece, to):
        return remote(
            big.at[t, x, piece],
            big.at[t, x, piece],
            bg_s.at[t, piece, to],
            bg_r.at[t, piece, x],
            ctx=4 * to + mine,
        )

    def sib_copy(t, piece):
        return remote(
            big.at[t, x, piece],
            big.at[t, 4, piece],
            bg_s.at[t, piece, x],
            bg_r.at[t, piece, 4],
            ctx=sibling,
        )

    def piece_wait(t, piece, slot):
        remote(
            big.at[t, x, piece],
            big.at[t, slot, piece],
            bg_s.at[t, piece, slot % 4],
            bg_r.at[t, piece, slot],
            ctx=sibling,
        ).wait_recv()

    def targets(t, body):
        if t in (Q, DO):
            loop(0, x, lambda i: body(x - 1 - i))
        else:
            loop(x + 1, NX, body)

    def send_x(t, piece):
        targets(t, lambda to: x_copy(t, piece, to).start())

    def send_piece(t, piece):
        sib_copy(t, piece).start()
        send_x(t, piece)

    def drain_piece(t, piece):
        sib_copy(t, piece).wait_send()
        targets(t, lambda to: x_copy(t, piece, to).wait_send())

    for load in loads[4:7]:
        load.wait()
    place(Q, query)
    place(DO, grad)
    place(K, key)
    rel[...] = (
        lax.broadcasted_iota(jnp.int32, (BLK, 2 * BLK), 1)
        + BLK * (lax.broadcasted_iota(jnp.int32, (BLK, 2 * BLK), 1) // BLK)
        + BLK * a
        - lax.broadcasted_iota(jnp.int32, (BLK, 2 * BLK), 0)
    )

    pl.semaphore_wait(barrier, n_ctx + n_tp - 2)

    swap_copy(Q).start()
    swap_copy(K).start()
    send_x(Q, y)
    sib_copy(K, y).start()
    loop(b + 1, n_ctx, lambda dst: state_copy(0, dst).start())
    swap_copy(DO).start()
    swap_wait(Q)
    send_x(Q, 1 - y)
    swap_wait(K)
    sib_copy(K, 1 - y).start()
    send_piece(DO, y)
    swap_wait(DO)
    send_piece(DO, 1 - y)
    for piece in (0, 1):
        sib_copy(Q, piece).start()

    def gather_states(way):
        def hop(i, total):
            src = n_ctx - 1 - i if way else i
            state_wait(way, src)
            return d256 * total + state_in[way, src].astype(F32)

        count = n_ctx - 1 - b if way else b
        ein[...] = lax.fori_loop(0, count, hop, jnp.zeros((MODES, 2 * HD), F32))

    def tp_copy(which, r):
        return remote(
            tp_out.at[which],
            tp_in.at[which, n_tp - 1 - r],
            tp_s.at[which],
            tp_r.at[which],
            tp=lax.rem(tp + r, n_tp),
        )

    def tp_all(which):
        return remote(
            tp_in.at[which], tp_in.at[which], tp_s.at[which], tp_r.at[which], tp=lax.rem(tp + 1, n_tp)
        )

    for load in loads[7:]:
        load.wait()
    gather_states(0)
    filter_run(False)
    total = stream[...].astype(F32) + gate[...].astype(F32) * jnp.concatenate(
        [conv[0:BLK, :], conv[BLK:, :]], axis=1
    )
    normed[...] = total
    tp_out[0] = row_sums(total * total)
    loop(1, n_tp, lambda r: tp_copy(0, r).start())
    for piece in (0, 1):
        send_x(K, piece)

    def chip_tile(t, r):
        return big[t, jnp.where(r % 2 == a, x, 4), r // 2]

    def x_tile(t, slot):
        return big[t, slot].reshape(2 * BLK, HD)

    neg = jnp.full((4, 2 * BLK), FILL, F32)
    ml[x, 0:4] = neg
    ml[x, 4:8] = jnp.zeros_like(neg)

    def key_scores(xq, own):
        queries = x_tile(Q, xq)
        top = jnp.full((1, 2 * BLK), FILL, F32)
        for r in range(4):
            s = dot_nt(chip_tile(K, r), queries) * (scale * LOG2E)
            if own:
                s = jnp.where(rel[...] >= BLK * r, s, FILL)
            work[r] = s
            top = jnp.maximum(top, jnp.max(s, axis=0, keepdims=True))
        total = jnp.zeros((1, 2 * BLK), F32)
        for r in range(4):
            e = jnp.exp2(work[r] - top)
            exps[xq, r] = e.astype(BF16)
            total = total + jnp.sum(e, axis=0, keepdims=True)
        ml[x, pl.ds(xq, 1)] = top
        ml[x, pl.ds(4 + xq, 1)] = total

    for piece in (0, 1):
        piece_wait(K, piece, 4)
    key_scores(x, True)

    def later_scores(xq):
        for piece in (0, 1):
            piece_wait(Q, piece, xq)
        key_scores(xq, False)

    loop(x + 1, NX, later_scores)

    def stat_copy(buf, send, recv, to):
        return remote(buf.at[x], buf.at[x], send.at[to], recv.at[x], ctx=4 * to + mine)

    def stat_wait(buf, send, recv, src):
        remote(buf.at[src], buf.at[src], send.at[src], recv.at[src], ctx=4 * src + mine).wait_recv()

    def others(body):
        loop(1, NX, lambda r: body(lax.rem(x + r, NX)))

    others(lambda to: stat_copy(ml, ml_s, ml_r, to).start())

    def tp_total(which):
        tp_all(which).wait_recv()
        return jnp.sum(tp_in[which], axis=0) + tp_out[which]

    inverse = columns(lax.rsqrt(tp_total(0) / float(n_tp * 2 * HD) + EPS))
    inv[...] = inverse
    normed[...] = normed[...] * jnp.concatenate([inverse, inverse], axis=1)
    swap[V] = jnp.zeros((BLK, HD), BF16)
    vals = (normed[...] * gain[...]).astype(BF16)

    @pl.when(y == 0)
    def _():
        big[V, x, 0] = vals[:, :HD]
        swap[V] = vals[:, HD:]

    @pl.when(y == 1)
    def _():
        big[V, x, 1] = vals[:, HD:]
        swap[V] = vals[:, :HD]

    swap_copy(V).start()
    remote(
        swap.at[V],
        big.at[V, 4, y],
        bg_s.at[V, 1 - y, x],
        bg_r.at[V, y, 4],
        ctx=across + 1 - 2 * a,
    ).start()
    send_piece(V, y)

    others(lambda src: stat_wait(ml, ml_s, ml_r, src))
    tops = jnp.max(ml[:, 0:4, :], axis=0)
    sums = jnp.sum(ml[:, 4:8, :] * jnp.exp2(ml[:, 0:4, :] - tops[None]), axis=0)
    lse = tops + jnp.log2(sums)
    fs[4:8] = lse
    fs[0:4] = jnp.exp2(ml[x, 0:4] - lse)

    def sib_stat(kind):
        return remote(ls.at[kind, 0], ls.at[kind, 1], ls_s.at[kind], ls_r.at[kind], ctx=sibling)

    ls[0, 0] = fs[pl.ds(4 + x, 1)]
    sib_stat(0).start()

    def scale_rows(xq):
        f = columns(fs[pl.ds(xq, 1)])
        dos[xq] = (x_tile(DO, xq).astype(F32) * f).astype(BF16)

    def later_rows(xq):
        for piece in (0, 1):
            piece_wait(DO, piece, xq)
        scale_rows(xq)

    scale_rows(x)
    loop(x + 1, NX, later_rows)

    def ret_copy(t, r):
        return remote(
            ret_out.at[t, r], ret_in.at[t, mine], rt_s.at[t, r], rt_r.at[t, mine], ctx=4 * x + r
        )

    def ret_wait(t, src):
        remote(
            ret_out.at[t, src], ret_in.at[t, src], rt_s.at[t, src], rt_r.at[t, src], ctx=4 * x + src
        ).wait_recv()

    def quad(body):
        loop(1, 4, lambda i: body(lax.rem(mine + i, 4)))

    def give_back(t, r, value):
        ret_out[t, r] = value.astype(BF16)

        @pl.when(r != mine)
        def _():
            ret_copy(t, r).start()

        @pl.when(r == mine)
        def _():
            ret_in[t, mine] = ret_out[t, mine]

    def take_back(t):
        quad(lambda src: ret_wait(t, src))
        return jnp.concatenate(
            [
                ret_in[t, 0].astype(F32) + ret_in[t, 1].astype(F32),
                ret_in[t, 2].astype(F32) + ret_in[t, 3].astype(F32),
            ],
            axis=1,
        )

    for row in (1 - y, y):

        def value_grads(xq):
            for r in (2 * row, 2 * row + 1):
                acc[0, r] = acc[0, r] + dot(exps[xq, r], dos[xq])

        for r in (2 * row, 2 * row + 1):
            acc[0, r] = dot(exps[x, r], dos[x])
        loop(x + 1, NX, value_grads)
        for r in (2 * row, 2 * row + 1):
            give_back(R_DV, r, acc[0, r])

    swap_wait(V)
    send_x(V, 1 - y)
    for piece in (0, 1):
        piece_wait(V, piece, 4)
    dl[x] = jnp.zeros((8, 2 * BLK), F32)

    def key_delta(xq):
        f = fs[pl.ds(xq, 1)]
        qs[xq] = (x_tile(Q, xq).astype(F32) * (columns(f) * scale)).astype(BF16)
        cotangents = x_tile(DO, xq)
        total = jnp.zeros((1, 2 * BLK), F32)
        for r in range(4):
            dp = dot_nt(chip_tile(V, r), cotangents)
            dprob[xq, r] = dp
            total = total + jnp.sum(exps[xq, r].astype(F32) * dp, axis=0, keepdims=True)
        dl[x, pl.ds(xq, 1)] = total * f

    loop(x, NX, key_delta)
    others(lambda to: stat_copy(dl, dl_s, dl_r, to).start())

    def wide(col):
        return jnp.concatenate([col] * 4, axis=1)

    def side(r):
        return jnp.where(r % 2 == a, 0, 1)

    sib_stat(0).wait_recv()
    for who in (0, 1):
        lcol[0, who] = columns(ls[0, who]).reshape(2, BLK, HD)
    for piece in (0, 1):
        piece_wait(Q, piece, 4)

    def query_probs(xk, own):
        keys = x_tile(K, xk)
        for r in range(4):
            s = dot_nt(chip_tile(Q, r), keys) * (scale * LOG2E)
            p = jnp.exp2(s - wide(lcol[0, side(r), r // 2]))
            if own:
                p = jnp.where(rel[...] <= BLK * r, p, 0.0)
            probs[xk, r] = p.astype(BF16)

    def earlier_probs(xk):
        for piece in (0, 1):
            piece_wait(K, piece, xk)
        query_probs(xk, False)

    query_probs(x, True)
    loop(0, x, earlier_probs)

    loop(b + 1, n_ctx, lambda dst: state_copy(0, dst).wait_send())
    for t in (Q, DO, K, V):
        swap_copy(t).wait_send()
    for t in (Q, DO, K):
        for piece in (0, 1):
            drain_piece(t, piece)
    tp_all(0).wait_send()
    sib_stat(0).wait_send()
    others(lambda to: stat_copy(ml, ml_s, ml_r, to).wait_send())

    dvalues = take_back(R_DV)
    dsum[...] = dvalues * gain[...]
    tp_out[1] = row_sums(dsum[...] * normed[...])
    loop(1, n_tp, lambda r: tp_copy(1, r).start())
    gain_out[...] = jnp.sum(dvalues * normed[...], axis=0, keepdims=True)

    def gain_copy(r):
        return remote(
            gain_out, gain_in.at[n_ctx - 1 - r], ga_s.at[0], ga_r.at[0], ctx=lax.rem(b + r, n_ctx)
        )

    loop(1, n_ctx, lambda r: gain_copy(r).start())

    others(lambda src: stat_wait(dl, dl_s, dl_r, src))
    fs[0:8] = jnp.sum(dl[...], axis=0)
    ls[1, 0] = fs[pl.ds(x, 1)]
    sib_stat(1).start()

    def key_grads(xq, first):
        delta = fs[pl.ds(xq, 1)]
        for r in range(4):
            ds = exps[xq, r].astype(F32) * (dprob[xq, r] - delta)
            part = dot(ds.astype(BF16), qs[xq])
            acc[0, r] = part if first else acc[0, r] + part

    sib_stat(1).wait_recv()
    for who in (0, 1):
        lcol[1, who] = columns(ls[1, who]).reshape(2, BLK, HD)
    for piece in (0, 1):
        piece_wait(DO, piece, 4)

    def query_rows(xk, own):
        keys = x_tile(K, xk)
        vals = x_tile(V, xk)
        for r in range(4):
            p = probs[xk, r]
            dp = dot_nt(chip_tile(DO, r), vals)
            ds = p.astype(F32) * (dp - wide(lcol[1, side(r), r // 2]))
            att = dot(p, vals)
            dq = dot(ds.astype(BF16), keys)
            acc[0, r] = att if own else acc[0, r] + att
            acc[1, r] = dq if own else acc[1, r] + dq

    def earlier_rows(xk):
        for piece in (0, 1):
            piece_wait(V, piece, xk)
        query_rows(xk, False)

    def all_key_grads():
        key_grads(x, True)
        loop(x + 1, NX, lambda xq: key_grads(xq, False))
        for r in range(4):
            give_back(R_DK, r, acc[0, r])

    def all_query_rows():
        query_rows(x, True)
        loop(0, x, earlier_rows)
        for r in range(4):
            give_back(R_ATT, r, acc[0, r])
            give_back(R_DQ, r, acc[1, r] * scale)

    all_query_rows()

    dot_col = columns(tp_total(1) / float(n_tp * 2 * HD))
    inverse2 = jnp.concatenate([inv[...], inv[...]], axis=1)
    dsummed = inverse2 * (dsum[...] - normed[...] * jnp.concatenate([dot_col, dot_col], axis=1))
    back = dsummed * gate[...].astype(F32)
    xs[0:BLK, :] = back[:, :HD]
    xs[BLK:, :] = back[:, HD:]
    filter_ends(True)
    loop(0, b, lambda dst: state_copy(1, dst).start())
    stream_o[...] = dsummed.astype(BF16)
    gate_o[...] = (
        dsummed * jnp.concatenate([conv[0:BLK, :], conv[BLK:, :]], axis=1)
    ).astype(BF16)
    stores[4].start()
    stores[1].start()

    all_key_grads()

    for piece in (0, 1):
        drain_piece(V, piece)
    tp_all(1).wait_send()
    sib_stat(1).wait_send()
    remote(gain_in, gain_in, ga_s.at[0], ga_r.at[0], ctx=sibling).wait_send()
    others(lambda to: stat_copy(dl, dl_s, dl_r, to).wait_send())
    quad(lambda r: ret_copy(R_DV, r).wait_send())

    gather_states(1)
    filter_run(True)
    dmixed = jnp.concatenate([conv[0:BLK, :], conv[BLK:, :]], axis=1)
    keyp_o[...] = (dmixed * valp[...].astype(F32)).astype(BF16)
    valp_o[...] = (dmixed * keyp[...].astype(F32)).astype(BF16)

    stores[2].start()
    stores[3].start()

    remote(gain_in, gain_in, ga_s.at[0], ga_r.at[0], ctx=sibling).wait_recv()
    gain_o[...] = jnp.sum(gain_in[...], axis=0) + gain_out[...]
    stores[5].start()
    key_o[...] = take_back(R_DK).astype(BF16)
    stores[7].start()
    att_o[...] = take_back(R_ATT).astype(BF16)
    stores[0].start()
    query_o[...] = take_back(R_DQ).astype(BF16)
    stores[6].start()

    loop(0, b, lambda dst: state_copy(1, dst).wait_send())
    for t in (R_DK, R_ATT, R_DQ):
        quad(lambda r: ret_copy(t, r).wait_send())
    for copy in stores:
        copy.wait()


def store(*refs):
    held, sem = refs[16:24], refs[24]
    arrive = [pltpu.make_async_copy(refs[i], held[i], sem.at[0, i]) for i in range(8)]
    leave = [pltpu.make_async_copy(held[i], refs[8 + i], sem.at[1, i]) for i in range(8)]
    for copy in arrive:
        copy.start()
    for one, other in zip(arrive, leave):
        one.wait()
        other.start()
    for copy in leave:
        copy.wait()


def on_device(n_ctx, n_tp, *arrays):
    (gate, keyp, valp, stream, decay, residue, gain, query, key, grad) = arrays
    rows, chans = stream.shape
    full = jax.ShapeDtypeStruct((rows, chans), BF16)
    dma = pltpu.SemaphoreType.DMA

    def body(*refs):
        kernel(n_ctx, n_tp, *refs)

    scratch = [
        *[pltpu.VMEM((rows, chans), BF16)] * 4,
        *[pltpu.VMEM((MODES, chans), F32)] * 2,
        pltpu.VMEM((1, chans), F32),
        *[pltpu.VMEM((rows, chans), BF16)] * 3,
        *[pltpu.VMEM((rows, chans), BF16)] * 5,
        pltpu.VMEM((1, chans), F32),
        *[pltpu.VMEM((rows, chans), BF16)] * 2,
        pltpu.VMEM((2 * BLK, HD), F32),
        pltpu.VMEM((2 * BLK, HD), F32),
        *[pltpu.VMEM((MODES, 8, HD), F32)] * 6,
        pltpu.VMEM((2, MODES, 2 * HD), BF16),
        pltpu.VMEM((2, n_ctx, MODES, 2 * HD), BF16),
        pltpu.VMEM((MODES, 2 * HD), F32),
        pltpu.VMEM((2, 1, BLK), F32),
        pltpu.VMEM((2, n_tp - 1, 1, BLK), F32),
        pltpu.VMEM((1, 2 * HD), F32),
        pltpu.VMEM((n_ctx - 1, 1, 2 * HD), F32),
        pltpu.VMEM((BLK, 2 * HD), F32),
        pltpu.VMEM((BLK, HD), F32),
        pltpu.VMEM((BLK, 2 * HD), F32),
        pltpu.VMEM((4, BLK, HD), BF16),
        pltpu.VMEM((4, 5, 2, BLK, HD), BF16),
        pltpu.VMEM((NX, 4, BLK, 2 * BLK), BF16),
        pltpu.VMEM((NX, 4, BLK, 2 * BLK), BF16),
        pltpu.VMEM((4, BLK, 2 * BLK), F32),
        pltpu.VMEM((NX, 4, BLK, 2 * BLK), F32),
        pltpu.VMEM((BLK, 2 * BLK), jnp.int32),
        pltpu.VMEM((NX, 8, 2 * BLK), F32),
        pltpu.VMEM((NX, 8, 2 * BLK), F32),
        pltpu.VMEM((8, 2 * BLK), F32),
        pltpu.VMEM((NX, 2 * BLK, HD), BF16),
        pltpu.VMEM((2, 4, BLK, HD), F32),
        pltpu.VMEM((NX, 2 * BLK, HD), BF16),
        pltpu.VMEM((2, 2, 1, 2 * BLK), F32),
        pltpu.VMEM((2, 2, 2, BLK, HD), F32),
        pltpu.VMEM((4, 4, BLK, HD), BF16),
        pltpu.VMEM((4, 4, BLK, HD), BF16),
        dma((2, n_ctx)),
        dma((2, n_ctx)),
        dma((2,)),
        dma((2,)),
        dma((1,)),
        dma((1,)),
        dma((4,)),
        dma((4,)),
        dma((4, 2, 4)),
        dma((4, 2, 5)),
        dma((NX,)),
        dma((NX,)),
        dma((NX,)),
        dma((NX,)),
        dma((2,)),
        dma((2,)),
        dma((4, 4)),
        dma((4, 4)),
        dma((10,)),
        dma((8,)),
    ]
    hbm = pl.BlockSpec(memory_space=pltpu.HBM)
    shapes = (full,) * 5 + (jax.ShapeDtypeStruct((1, chans), F32),) + (full,) * 2
    outs = pl.pallas_call(
        body,
        out_shape=shapes,
        in_specs=[hbm] * 10,
        out_specs=(hbm,) * 8,
        scratch_shapes=scratch,
        compiler_params=pltpu.CompilerParams(
            collective_id=0, has_side_effects=True, vmem_limit_bytes=VMEM
        ),
    )(gate, keyp, valp, stream, decay, residue, gain.reshape(1, chans), query, key, grad)
    outs = pl.pallas_call(
        store,
        out_shape=shapes,
        in_specs=[hbm] * 8,
        out_specs=(hbm,) * 8,
        scratch_shapes=[*[pltpu.VMEM(s.shape, s.dtype) for s in shapes], dma((2, 8))],
        compiler_params=pltpu.CompilerParams(vmem_limit_bytes=VMEM),
    )(*outs)
    return outs[:5] + (outs[5].reshape(chans),) + outs[6:]


def solution(mesh):
    n_ctx, n_tp = mesh.shape["ctx"], mesh.shape["tp"]
    both = P("ctx", "tp")

    def body(*arrays):
        return on_device(n_ctx, n_tp, *arrays)

    return jax.shard_map(
        body,
        mesh=mesh,
        in_specs=(both,) * 4 + (P(None, "tp"), P(None, "tp"), P("tp")) + (both,) * 3,
        out_specs=(both,) * 5 + (P("tp"),) + (both,) * 2,
        check_vma=False,
    )
```
